512 devices in a mesh: row: 128 (over y, z, core), lm: 4 (over x).
Axes of the slice: x: 4, y: 8, z: 8, core: 2. Of those that a mesh axis runs over, the one named last changes fastest.
Arguments:
- state: float32 [3, 2048, 1024], P(None, 'row', 'lm'), may hold values from -6 to 6
- previous_terms: float32 [3, 2048, 1024], P(None, 'row', 'lm'), may hold values from -6 to 6
- below: float32 [2, 3, 1024], P(None, None, 'lm'), may hold values from -6 to 6
- above: float32 [2, 3, 1024], P(None, None, 'lm'), may hold values from -6 to 6
- kappa: float32 [3], replicated, may hold values from 0.25 to 1
Outputs:
- new_state: float32 [3, 2048, 1024], P(None, 'row', 'lm')
- nonlinear: float32 [3, 2048, 1024], P(None, 'row', 'lm')
The draws below stay inside these ranges and needn't reach their ends.
All inputs are finite; a program needn't handle non-finite values.
Results may differ from the reference program's by a relative error of at most 0.0006.
Values sent between devices are 32-bit elements; how exact they have to be, the bound alone decides.
A program may use at most 64 MiB of HBM per device.

```python
import math
import jax
import jax.numpy as jnp
from jax import lax

L = 1024
NLAT = 1536
FIELDS = 3
SHELLS_DEV = 16
SHELLS = 2048


def shard_levels(own_key, dims, cuts, smallest, high):
    def one(dim, shards_of):
        draws = jax.random.uniform(jax.random.fold_in(jax.random.fold_in(own_key, 6), dim), (shards_of,), jnp.float32, smallest / len(cuts), high / len(cuts))
        return jnp.repeat(jnp.exp(draws), dims[dim] // shards_of).reshape((-1,) + (1,) * (len(dims) - dim - 1))

    level = one(*cuts[0])
    for cut in cuts[1:]:
        level = level * one(*cut)
    return level


def bell_draw(rng, shape, deviation, bound, pieces=(), kind=jnp.bfloat16):
    array = jax.random.normal(rng, shape, jnp.float32) * deviation
    if len(pieces) > 0:
        array = shard_levels(rng, shape, pieces, -0.22, 0.18) * array
    return jnp.clip(array, min=-bound, max=bound).astype(kind)


def setup_inputs(seed: int = 0) -> dict:
    keys = jax.random.split(jax.random.key(seed), 6)
    return {
        "state": bell_draw(keys[0], (FIELDS, SHELLS, L), 1.0, 6.0, ((1, 128), (2, 4)), jnp.float32),
        "previous_terms": bell_draw(keys[1], (FIELDS, SHELLS, L), 1.0, 6.0, ((1, 128), (2, 4)), jnp.float32),
        "below": bell_draw(keys[2], (2, FIELDS, L), 1.0, 6.0, ((2, 4),), jnp.float32),
        "above": bell_draw(keys[3], (2, FIELDS, L), 1.0, 6.0, ((2, 4),), jnp.float32),
        "kappa": jnp.clip(jnp.exp(jax.random.uniform(keys[4], (FIELDS,), jnp.float32, math.log(0.25), math.log(1.0))), 0.25, 1.0),
    }


highest = lax.Precision.HIGHEST
CENTRAL_TERMS = [math.comb(2 * member, member) / 4.0 ** member for member in range(16)]

def central_ratio(counts):
    number = counts.astype(jnp.float32)
    bigger = jnp.maximum(number, 1.0)
    inverse = 1.0 / bigger
    series = 1.0 + inverse * (-0.125 + inverse * (0.0078125 + inverse * (0.0048828125 - inverse * 0.000640869140625)))
    result = series / jnp.sqrt(math.pi * bigger)
    for member in range(16):
        result = jnp.where(counts == member, CENTRAL_TERMS[member], result)
    return result

def expansion(degrees, orders):
    offsets = degrees - orders
    usable = (offsets >= 0) & (offsets % 2 == 0)
    lower_index = jnp.where(usable, offsets // 2, 0)
    upper_index = jnp.where(usable, (degrees + orders) // 2, 0)
    doubled = jnp.where(orders > 0, 2.0, 1.0)
    values = doubled * central_ratio(lower_index) * central_ratio(upper_index) * jnp.sqrt(degrees.astype(jnp.float32) + 0.5)
    return jnp.where(usable, values, 0.0).astype(jnp.float32)

def cosines(orders, thetas, nlat_count):
    phases = orders * (2 * thetas + 1) % (4 * nlat_count)
    return jnp.cos(phases.astype(jnp.float32) * (math.pi / (2 * nlat_count)))

def fejer_weights(thetas, nlat_count):
    orders = jnp.arange(1, nlat_count // 2 + 1, dtype=jnp.int32)[:, None]
    phases = orders * (2 * thetas[None, :] + 1) % (2 * nlat_count)
    order_values = orders.astype(jnp.float32)
    terms = jnp.cos(phases.astype(jnp.float32) * (math.pi / nlat_count)) / (4.0 * order_values * order_values - 1.0)
    return 2.0 / nlat_count * (1.0 - 2.0 * lax.optimization_barrier(jnp.sum(terms, axis=0)))

def radial_terms(kappa, shell_ids, degree_ids, shells_all, shells_dev):
    radius = 0.5 + (shell_ids.astype(jnp.float32) + 0.5) / (2.0 * shells_all)
    slope = 1.0 / (2.0 * shells_all * radius)
    spread = kappa[:, None, None] * (16.0 * shells_dev * shells_dev)
    degree = degree_ids.astype(jnp.float32)
    damping = kappa[:, None, None] * (degree * (degree + 1.0))[None, None, :] / (256.0 * radius * radius)[None, :, None]
    diagonal = 1.0 + 2.0 * spread + damping
    keeping = 1.0 - 2.0 * spread - damping
    full_shape = diagonal.shape
    lower = jnp.broadcast_to(spread * (1.0 - slope)[None, :, None], full_shape)
    upper = jnp.broadcast_to(spread * (1.0 + slope)[None, :, None], full_shape)
    return (diagonal, lower, upper, keeping)

def products_of(grid_values):
    velocity = grid_values[0]
    magnetic = grid_values[1]
    thermal = grid_values[2]
    return jnp.stack([(magnetic * magnetic - velocity * velocity) / 16.0, velocity * magnetic / 16.0, -velocity * thermal / 16.0])

def reference(state, previous_terms, below, above, kappa):
    shells_all = state.shape[1]
    degrees_all = state.shape[2]
    shells_dev = SHELLS_DEV
    degree_ids = jnp.arange(degrees_all, dtype=jnp.int32)
    theta_ids = jnp.arange(NLAT, dtype=jnp.int32)
    legendre = jnp.dot(expansion(degree_ids[:, None], degree_ids[None, :]), cosines(degree_ids[:, None], theta_ids[None, :], NLAT), precision=highest, preferred_element_type=jnp.float32)
    weights = fejer_weights(theta_ids, NLAT)
    grid_values = jnp.einsum('fsl,lt->fst', state, legendre, precision=highest)
    weighted = products_of(grid_values) * weights
    nonlinear = jnp.einsum('fst,lt->fsl', weighted, legendre, precision=highest)
    diagonal, lower, upper, keeping = radial_terms(kappa, jnp.arange(shells_all, dtype=jnp.int32), degree_ids, shells_all, shells_dev)
    forcing = 4.0 * shells_dev * shells_dev * (1.5 * nonlinear - 0.5 * previous_terms)
    below_old = jnp.concatenate([below[0][:, None, :], state[:, :-1]], axis=1)
    above_old = jnp.concatenate([state[:, 1:], above[0][:, None, :]], axis=1)
    right_side = keeping * state + upper * above_old + lower * below_old + forcing

    def forward(carried, inputs):
        coupling, offset = carried
        diag_now, low_now, high_now, side_now = inputs
        pivots = diag_now - low_now * coupling
        new_coupling = high_now / pivots
        new_offset = (side_now + low_now * offset) / pivots
        return ((new_coupling, new_offset), (new_coupling, new_offset))
    moved = tuple((jnp.moveaxis(member, 1, 0) for member in (diagonal, lower, upper, right_side)))
    starting = (jnp.zeros_like(below[1]), below[1])
    ignored, sweeps = lax.scan(forward, starting, moved)

    def backward(upper_value, inputs):
        coupling, offset = inputs
        value = coupling * upper_value + offset
        return (value, value)
    ignored_last, solved = lax.scan(backward, above[1], sweeps, reverse=True)
    new_state = jnp.moveaxis(solved, 0, 1)
    return (new_state, nonlinear)
```

```python
import functools
import math

import jax
import jax.numpy as jnp
from jax import lax
from jax.experimental import pallas as pl
from jax.experimental.pallas import tpu as pltpu
from jax.sharding import PartitionSpec as P

MESH = pl.DeviceIdType.MESH
F32, BF16 = jnp.float32, jnp.bfloat16
NLAT = 1536
HALF = NLAT // 2
DEGREES = 1024
PAIRS = DEGREES // 2
SHELLS = 2048
SHELLS_DEV = 16
CHIP = 2 * SHELLS_DEV
FIELDS = 3
TILE = (8, 128)
CENTRAL_TERMS = [math.comb(2 * k, k) / 4.0**k for k in range(16)]


def central_ratio(counts):
    number = counts.astype(F32)
    bigger = jnp.maximum(number, 1.0)
    inverse = 1.0 / bigger
    series = 1.0 + inverse * (
        -0.125 + inverse * (0.0078125 + inverse * (0.0048828125 - inverse * 0.000640869140625))
    )
    result = series * lax.rsqrt(math.pi * bigger)
    for k in range(16):
        result = jnp.where(counts == k, CENTRAL_TERMS[k], result)
    return jnp.where(counts < 0, 0.0, result)


def cosine(phase):
    turn = 4.0 * NLAT
    number = phase.astype(F32)
    number = number - turn * jnp.floor(number * (1.0 / turn) + 0.5)
    angle = (NLAT - jnp.abs(number)) * (math.pi / (2 * NLAT))
    square = angle * angle
    total = jnp.full_like(square, 1.0 / math.factorial(13))
    for order in (11, 9, 7, 5, 3, 1):
        sign = -1.0 if order % 4 == 3 else 1.0
        total = sign / math.factorial(order) + square * total
    return angle * total


def split2(value):
    high = value.astype(BF16)
    low = (value - high.astype(F32)).astype(BF16)
    return high, low


def dot(left, right, transposed=False):
    dims = (((1,), (1 if transposed else 0,)), ((), ()))
    return lax.dot_general(left, right, dims, preferred_element_type=F32)


def dot3(left, high, low, transposed=False):
    rows = left.shape[0]
    top, rest = split2(left)
    both = dot(jnp.concatenate([top, rest], axis=0), high, transposed)
    return both[:rows] + both[rows:] + dot(top, low, transposed)


def permute_lanes(value, matrix):
    rows = value.shape[0]
    first = value.astype(BF16)
    left = value - first.astype(F32)
    second = left.astype(BF16)
    third = (left - second.astype(F32)).astype(BF16)
    out = dot(jnp.concatenate([first, second, third], axis=0), matrix)
    return out[:rows] + out[rows : 2 * rows] + out[2 * rows :]


def iota(shape, axis):
    return lax.broadcasted_iota(jnp.int32, shape, axis)


def level_parts(ports, own):
    count = len(ports)
    one, nothing = jnp.ones(TILE, F32), jnp.zeros(TILE, F32)

    def pick(place, new, old):
        return jnp.where(own == place, new, old)

    forward, backward = [None] * count, [None] * count
    a1, b1 = one, nothing
    pre_a1, pre_b1, thru_a1, thru_b1 = one, nothing, one, nothing
    for k in range(count):
        pa0, pb0, pa1, pb1 = ports[k]
        pre_a1, pre_b1 = pick(k, a1, pre_a1), pick(k, b1, pre_b1)
        beta = pa1 / (1.0 - b1 * pa0)
        forward[k] = (beta, beta * b1)
        a1, b1 = beta * a1, pb1 + beta * b1 * pb0
        thru_a1, thru_b1 = pick(k, a1, thru_a1), pick(k, b1, thru_b1)
    a0, b0 = nothing, one
    post_a0, post_b0, from_a0, from_b0 = nothing, one, nothing, one
    for k in reversed(range(count)):
        pa0, pb0, pa1, pb1 = ports[k]
        post_a0, post_b0 = pick(k, a0, post_a0), pick(k, b0, post_b0)
        gamma = pb0 / (1.0 - pb1 * a0)
        backward[k] = (gamma, gamma * a0)
        a0, b0 = pa0 + gamma * a0 * pa1, gamma * b0
        from_a0, from_b0 = pick(k, a0, from_a0), pick(k, b0, from_b0)
    lower_scale = 1.0 / (1.0 - pre_b1 * from_a0)
    upper_scale = 1.0 / (1.0 - post_a0 * thru_b1)
    lower = (lower_scale * pre_a1, lower_scale * pre_b1 * from_b0, lower_scale * pre_b1, lower_scale)
    upper = (
        upper_scale * post_a0 * thru_a1,
        upper_scale * post_b0,
        upper_scale * post_a0,
        upper_scale,
    )
    return forward, backward, lower, upper, (a0, b0, a1, b1)


def level_constants(parts, constants, own):
    forward, backward, lower, upper, _ = parts
    count = len(forward)
    nothing = jnp.zeros(TILE, F32)

    def pick(place, new, old):
        return jnp.where(own == place, new, old)

    c1, pre, thru = nothing, nothing, nothing
    for k in range(count):
        k0, k1 = constants[k]
        pre = pick(k, c1, pre)
        beta, beta_b = forward[k]
        c1 = (k1 + beta_b * k0) + beta * c1
        thru = pick(k, c1, thru)
    c0, post, start = nothing, nothing, nothing
    for k in reversed(range(count)):
        k0, k1 = constants[k]
        post = pick(k, c0, post)
        gamma, gamma_a = backward[k]
        c0 = (k0 + gamma_a * k1) + gamma * c0
        start = pick(k, c0, start)
    return c0, c1, lower[2] * start + lower[3] * pre, upper[2] * thru + upper[3] * post


def kernel(
    state_hbm,
    previous_hbm,
    below_hbm,
    above_hbm,
    kappa_hbm,
    new_ref,
    nonlinear_ref,
    state_raw,
    previous_raw,
    sides_raw,
    kappa_ref,
    mix,
    wide,
    tri_x,
    sent_x,
    got_x,
    forcing,
    ports_t,
    ports_h,
    exp_high,
    exp_low,
    angle_cos,
    angle_sin,
    cos_high,
    cos_low,
    sent_n,
    got_n,
    radial,
    green,
    solved,
    port_z,
    port_y,
    const_z,
    const_y,
    load_sem,
    x_send,
    x_recv,
    n_send,
    n_recv,
    u_send,
    u_recv,
    pz_send,
    pz_recv,
    py_send,
    py_recv,
    cz_send,
    cz_recv,
    cy_send,
    cy_recv,
):
    row, mode = lax.axis_index("row"), lax.axis_index("lm")
    y, z, core = row // 16, lax.rem(row // 2, 8), lax.rem(row, 2)
    other = row + 1 - 2 * core
    turn = [lax.rem(mode + d, 4) for d in range(4)]
    x_peers = [(row, turn[d]) for d in range(1, 4)]
    core_peers = [(other, turn[d]) for d in range(4)]
    z_peers = [(y * 16 + lax.rem(z + d, 8) * 2 + core, mode) for d in (4, 3, 5, 2, 6, 1, 7)]
    y_peers = [(lax.rem(y + d, 8) * 16 + z * 2 + core, mode) for d in (4, 3, 5, 2, 6, 1, 7)]

    barrier = pltpu.get_barrier_semaphore()
    everyone = z_peers + y_peers + x_peers + core_peers
    for peer in everyone:
        pl.semaphore_signal(barrier, inc=1, device_id=peer, device_id_type=MESH)

    loads = [
        pltpu.make_async_copy(state_hbm, state_raw, load_sem.at[0]),
        pltpu.make_async_copy(previous_hbm, previous_raw, load_sem.at[1]),
        pltpu.make_async_copy(below_hbm, sides_raw.at[0], load_sem.at[2]),
        pltpu.make_async_copy(above_hbm, sides_raw.at[1], load_sem.at[3]),
        pltpu.make_async_copy(kappa_hbm, kappa_ref, load_sem.at[4]),
    ]
    for load in loads:
        load.start()

    def send(source, target, send_sem, recv_sem, peer):
        copy = pltpu.make_async_remote_copy(
            src_ref=source,
            dst_ref=target,
            send_sem=send_sem,
            recv_sem=recv_sem,
            device_id=peer,
            device_id_type=MESH,
        )
        copy.start()
        return copy

    source_id, target_id = iota((256, 256), 0), iota((256, 256), 1)
    part = (source_id == 2 * (target_id & 127) + (target_id >> 7)).astype(F32).astype(BF16)
    unite = (target_id == 2 * (source_id & 127) + (source_id >> 7)).astype(F32).astype(BF16)
    sub, lane = iota(TILE, 0), iota(TILE, 1)
    parity, field = sub >> 2, sub & 3
    degree = (mode * 256 + 2 * lane + parity).astype(F32)
    scale = jnp.sqrt(degree + 0.5)

    def to_tiles(values, target):
        for f in range(FIELDS):
            for p in range(2):
                target[pl.ds(p * 4 + f, SHELLS_DEV, stride=8), :] = values[
                    f * 16 : (f + 1) * 16, p * 128 : (p + 1) * 128
                ]

    def from_tiles(source):
        return jnp.concatenate(
            [
                jnp.concatenate(
                    [source[pl.ds(p * 4 + f, SHELLS_DEV, stride=8), :] for p in range(2)], axis=1
                )
                for f in range(FIELDS)
            ],
            axis=0,
        )

    tri_x[...] = jnp.zeros_like(tri_x)
    wide[...] = jnp.zeros_like(wide)
    loads[0].wait()
    to_tiles(permute_lanes(state_raw[...].reshape(48, 256), part), tri_x)
    sent_x[...] = tri_x[...].reshape(SHELLS_DEV, 8, 128) * scale
    pl.semaphore_wait(barrier, len(everyone))
    copies_x = [
        send(
            sent_x.at[pl.ds(peer[1] * 4, 4)],
            got_x.at[mode],
            x_send.at[d],
            x_recv.at[d],
            peer,
        )
        for d, peer in enumerate(x_peers)
    ]
    got_x[mode] = sent_x[pl.ds(mode * 4, 4)]

    loads[1].wait()
    to_tiles(permute_lanes(previous_raw[...].reshape(48, 256), part), wide)
    push = 4.0 * SHELLS_DEV * SHELLS_DEV
    forcing[pl.ds(core * SHELLS_DEV, SHELLS_DEV)] = (
        2.0 * tri_x[...] - (0.5 * push) * wide[...]
    ).reshape(SHELLS_DEV, 8, 128)
    copy_u = send(
        forcing.at[pl.ds(core * SHELLS_DEV, SHELLS_DEV)],
        forcing.at[pl.ds(core * SHELLS_DEV, SHELLS_DEV)],
        u_send.at[0],
        u_recv.at[0],
        core_peers[0],
    )

    toeplitz = central_ratio(512 + iota((8, 640), 0) - iota((8, 640), 1))
    hankel = [central_ratio(iota((8, 1024), 0) + iota((8, 1024), 1) + p) for p in range(2)]
    for step in range(16):
        rows = slice(step * 8, step * 8 + 8)
        moved = toeplitz if step == 0 else pltpu.roll(toeplitz, step * 8, 1)
        for b in range(4):
            ports_t[b, rows, :] = moved[:, (4 - b) * 128 : (5 - b) * 128]
        for p in range(2):
            moved = hankel[p] if step == 0 else pltpu.roll(hankel[p], 1024 - step * 8, 1)
            for b in range(7):
                ports_h[p, b, rows, :] = moved[:, b * 128 : (b + 1) * 128]
    for p in range(2):
        for a in range(4):
            for b in range(4):
                here = (p, slice(a * 128, a * 128 + 128), slice(b * 128, b * 128 + 128))
                if b <= a:
                    high, low = split2(ports_t[a - b] * ports_h[p, a + b])
                else:
                    high = low = jnp.zeros((128, 128), BF16)
                exp_high[here] = high
                exp_low[here] = low

    def phase(order, shape):
        return order * (2 * iota(shape, 1) + 1)

    wide_shape = (8, HALF)
    for p, groups in ((0, 7), (1, 4)):
        for group in range(groups):
            turns = phase(32 * (group * 8 + iota(wide_shape, 0)) + p, wide_shape)
            angle_cos[p, group * 8 : group * 8 + 8, :] = 2.0 * cosine(turns)
            angle_sin[p, group * 8 : group * 8 + 8, :] = 2.0 * cosine(turns - NLAT)
    base_shape = (16, HALF)
    turns = phase(2 * iota(base_shape, 0), base_shape)
    base_cos, base_sin = cosine(turns), cosine(turns - NLAT)
    base_row = iota((16, 128), 0)

    def series_term(q):
        order = (16 * q + base_row).astype(F32)
        term = -1.0 / (4.0 * order * order - 1.0)
        term = jnp.where(order > HALF, 0.0, term)
        return jnp.concatenate([term] * (HALF // 128), axis=1)

    def table_rows(p, q):
        return (
            angle_cos[p, pl.ds(q, 1), :] * base_cos - angle_sin[p, pl.ds(q, 1), :] * base_sin
        )

    def fill(q, weight):
        for p in range(2):
            values = table_rows(p, q)
            if p == 0:
                values = jnp.where((iota(base_shape, 0) + 16 * q) == 0, 1.0, values)
                weight = weight + series_term(q) * values
            high, low = split2(values)
            where = pl.ds(pl.multiple_of(q * 16, 16), 16)
            cos_high[p, where, :] = high
            cos_low[p, where, :] = low
        return weight

    weight = lax.fori_loop(0, 32, fill, jnp.zeros(base_shape, F32))
    weight = lax.fori_loop(
        32, 49, lambda q, weight: weight + series_term(q) * table_rows(0, q), weight
    )
    weight = jnp.sum(weight, axis=0, keepdims=True) * (2.0 / NLAT / 16.0)

    for copy in copies_x:
        copy.wait_recv()
    even_rows = (iota((32, 1), 0) & 4) == 0
    field_rows = iota((32, 1), 0) & 3
    sign = jnp.where(even_rows, 1.0, -1.0)

    def parities(left, right):
        return jnp.where(even_rows, left, right)

    def swap(values):
        return pltpu.roll(values.reshape(4, 8, values.shape[1]), 4, 1).reshape(values.shape)

    def rolled(values, shift):
        return pltpu.roll(values.reshape(4, 8, values.shape[1]), shift, 1).reshape(values.shape)

    spectrum = jnp.concatenate([got_x[k].reshape(32, 128) for k in range(4)], axis=1)
    half = PAIRS // 2

    def expand(p):
        first = dot3(spectrum, exp_high[p, :, :half], exp_low[p, :, :half])
        second = dot3(spectrum[:, half:], exp_high[p, half:, half:], exp_low[p, half:, half:])
        return jnp.concatenate([first, second], axis=1)

    orders = parities(expand(0), expand(1))
    sides = parities(*[dot3(orders, cos_high[p], cos_low[p]) for p in range(2)])
    grid = swap(sides) + sign * sides
    after, before, twice = rolled(grid, 7), rolled(grid, 1), rolled(grid, 2)
    product = jnp.where(
        field_rows == 0,
        after * after - grid * grid,
        jnp.where(field_rows == 1, before * grid, jnp.where(field_rows == 2, -(twice * grid), 0.0)),
    )
    product = product * weight
    folded = swap(product) + sign * product
    orders = parities(*[dot3(folded, cos_high[p], cos_low[p], True) for p in range(2)])

    def contract(p):
        first = dot3(orders[:, :half], exp_high[p, :half, :half], exp_low[p, :half, :half], True)
        second = dot3(orders, exp_high[p, half:, :], exp_low[p, half:, :], True)
        return jnp.concatenate([first, second], axis=1)

    terms = parities(contract(0), contract(1))
    for k in range(4):
        sent_n[k] = terms[:, k * 128 : (k + 1) * 128].reshape(4, 8, 128)
    mine = core * 4 + mode
    copies_n = [
        send(sent_n.at[peer[1]], got_n.at[mine], n_send.at[d], n_recv.at[d], peer)
        for d, peer in enumerate(x_peers + core_peers)
    ]
    got_n[mine] = sent_n[mode]

    loads[4].wait()
    kappa = jnp.full(TILE, 1.0, F32)
    for f in range(FIELDS):
        kappa = jnp.where(field == f, kappa_ref[f], kappa)
    spread = kappa * (16.0 * SHELLS_DEV * SHELLS_DEV)
    damping = kappa * (degree * (degree + 1.0)) * (1.0 / 256.0)
    first_shell = (row // 2) * CHIP
    for s in range(CHIP):
        number = jnp.full(TILE, (first_shell + s).astype(F32), F32)
        inverse = 1.0 / (0.5 + (number + 0.5) / (2.0 * SHELLS))
        slope = spread * (inverse * (1.0 / (2.0 * SHELLS)))
        radial[0, s] = (1.0 + 2.0 * spread) + damping * inverse * inverse
        radial[1, s] = spread - slope
        radial[2, s] = spread + slope
    cp, cq = jnp.zeros(TILE, F32), jnp.zeros(TILE, F32)
    for s in range(CHIP):
        t = CHIP - 1 - s
        ip = 1.0 / (radial[0, s] - radial[1, s] * cp)
        cp = radial[2, s] * ip
        radial[3, s], radial[4, s] = cp, ip
        iq = 1.0 / (radial[0, t] - radial[2, t] * cq)
        cq = radial[1, t] * iq
        radial[5, t], radial[6, t] = cq, iq
    low_run = up_run = head_run = tail_run = jnp.ones(TILE, F32)
    for s in range(CHIP):
        t = CHIP - 1 - s
        iq, ip = radial[6, s], radial[4, t]
        green[0, s] = iq * head_run
        head_run = head_run * (radial[2, s] * iq)
        low_run = low_run * radial[5, s]
        green[2, s] = low_run
        green[1, t] = ip * tail_run
        tail_run = tail_run * (radial[1, t] * ip)
        up_run = up_run * radial[3, t]
        green[3, t] = up_run
    port_z[z, 0], port_z[z, 1] = green[2, 0], green[3, 0]
    port_z[z, 2], port_z[z, 3] = green[2, CHIP - 1], green[3, CHIP - 1]
    copies_pz = [
        send(port_z.at[z], port_z.at[z], pz_send.at[d], pz_recv.at[d], peer)
        for d, peer in enumerate(z_peers)
    ]

    loads[2].wait()
    loads[3].wait()
    mix[...] = jnp.zeros_like(mix)
    for k in range(2):
        mix[k * 8 : k * 8 + FIELDS, :] = sides_raw[k, 0] + sides_raw[k, 1]
    parted = permute_lanes(mix[...], part)
    bottom, top = [
        jnp.concatenate([parted[k * 8 : k * 8 + 4, :128], parted[k * 8 : k * 8 + 4, 128:]], axis=0)
        for k in range(2)
    ]

    copy_u.wait_recv()
    for copy in copies_n:
        copy.wait_recv()
    factor = (1.5 * push) * scale
    sums = [[None] * 4, [None] * 4]
    for s in range(CHIP):
        value = forcing[s] + factor * got_n[s // 4, s % 4]
        solved[s] = value
        for k in range(2):
            term = green[k, s] * value
            old = sums[k][s % 4]
            sums[k][s % 4] = term if old is None else old + term
    for k in range(2):
        const_z[z, k] = (sums[k][0] + sums[k][1]) + (sums[k][2] + sums[k][3])
    copies_cz = [
        send(const_z.at[z], const_z.at[z], cz_send.at[d], cz_recv.at[d], peer)
        for d, peer in enumerate(z_peers)
    ]

    for copy in copies_pz:
        copy.wait_recv()
    parts_z = level_parts([tuple(port_z[k, m] for m in range(4)) for k in range(8)], z)
    for m in range(4):
        port_y[y, m] = parts_z[4][m]
    copies_py = [
        send(port_y.at[y], port_y.at[y], py_send.at[d], py_recv.at[d], peer)
        for d, peer in enumerate(y_peers)
    ]

    run = jnp.zeros(TILE, F32)
    for s in range(CHIP):
        ip = radial[4, s]
        run = solved[s] * ip + (radial[1, s] * ip) * run
        solved[s] = run
    run = jnp.zeros(TILE, F32)
    for s in reversed(range(CHIP)):
        run = solved[s] + radial[3, s] * run
        solved[s] = run
    for q in range(4):
        wide[q * 32 : (q + 1) * 32, :] = (got_n[core * 4 + q] * scale).reshape(32, 128)
    nonlinear_ref[...] = permute_lanes(from_tiles(wide), unite).reshape(FIELDS, SHELLS_DEV, 256)

    for copy in copies_cz:
        copy.wait_recv()
    total0, total1, lower_z, upper_z = level_constants(
        parts_z, [(const_z[k, 0], const_z[k, 1]) for k in range(8)], z
    )
    const_y[y, 0], const_y[y, 1] = total0, total1
    copies_cy = [
        send(const_y.at[y], const_y.at[y], cy_send.at[d], cy_recv.at[d], peer)
        for d, peer in enumerate(y_peers)
    ]

    for copy in copies_py:
        copy.wait_recv()
    parts_y = level_parts([tuple(port_y[k, m] for m in range(4)) for k in range(8)], y)
    own_shells = pl.ds(core * SHELLS_DEV, SHELLS_DEV)
    rest = solved[own_shells] - tri_x[...].reshape(SHELLS_DEV, 8, 128)
    from_low, from_up = green[2, own_shells], green[3, own_shells]

    for copy in copies_cy:
        copy.wait_recv()
    _, _, lower_y, upper_y = level_constants(
        parts_y, [(const_y[k, 0], const_y[k, 1]) for k in range(8)], y
    )
    line_low = parts_y[2][0] * bottom + parts_y[2][1] * top + lower_y
    line_up = parts_y[3][0] * bottom + parts_y[3][1] * top + upper_y
    chip_low = parts_z[2][0] * line_low + parts_z[2][1] * line_up + lower_z
    chip_up = parts_z[3][0] * line_low + parts_z[3][1] * line_up + upper_z
    wide[...] = (rest + from_low * chip_low + from_up * chip_up).reshape(128, 128)
    new_ref[...] = permute_lanes(from_tiles(wide), unite).reshape(FIELDS, SHELLS_DEV, 256)

    for copy in copies_x + copies_n + [copy_u] + copies_pz + copies_py + copies_cz + copies_cy:
        copy.wait_send()


def local(state, previous_terms, below, above, kappa):
    block = jax.ShapeDtypeStruct(state.shape, F32)
    vmem, dma = pltpu.VMEM, pltpu.SemaphoreType.DMA
    anywhere = pl.BlockSpec(memory_space=pl.ANY)
    inside = pl.BlockSpec(memory_space=pltpu.VMEM)
    scratch = [
        vmem((FIELDS, SHELLS_DEV, 256), F32),
        vmem((FIELDS, SHELLS_DEV, 256), F32),
        vmem((2, 2, FIELDS, 256), F32),
        pltpu.SMEM((FIELDS,), F32),
        vmem((16, 256), F32),
        vmem((128, 128), F32),
        vmem((128, 128), F32),
        vmem((16, 8, 128), F32),
        vmem((4, 4, 8, 128), F32),
        vmem((CHIP, 8, 128), F32),
        vmem((4, 128, 128), F32),
        vmem((2, 7, 128, 128), F32),
        vmem((2, PAIRS, PAIRS), BF16),
        vmem((2, PAIRS, PAIRS), BF16),
        vmem((2, 56, HALF), F32),
        vmem((2, 56, HALF), F32),
        vmem((2, PAIRS, HALF), BF16),
        vmem((2, PAIRS, HALF), BF16),
        vmem((4, 4, 8, 128), F32),
        vmem((8, 4, 8, 128), F32),
        vmem((7, CHIP, 8, 128), F32),
        vmem((4, CHIP, 8, 128), F32),
        vmem((CHIP, 8, 128), F32),
        vmem((8, 4, 8, 128), F32),
        vmem((8, 4, 8, 128), F32),
        vmem((8, 2, 8, 128), F32),
        vmem((8, 2, 8, 128), F32),
        dma((5,)),
        dma((3,)),
        dma((3,)),
        dma((7,)),
        dma((7,)),
        dma((1,)),
        dma((1,)),
    ] + [dma((7,))] * 8
    return pl.pallas_call(
        kernel,
        out_shape=(block, block),
        in_specs=[anywhere] * 5,
        out_specs=(inside, inside),
        scratch_shapes=scratch,
        compiler_params=pltpu.CompilerParams(
            collective_id=0, has_side_effects=True, vmem_limit_bytes=32 * 1024 * 1024
        ),
    )(state, previous_terms, below, above, kappa)


def solution(mesh):
    in_specs = (
        P(None, "row", "lm"),
        P(None, "row", "lm"),
        P(None, None, "lm"),
        P(None, None, "lm"),
        P(),
    )
    out_specs = (P(None, "row", "lm"), P(None, "row", "lm"))
    return jax.shard_map(local, mesh=mesh, in_specs=in_specs, out_specs=out_specs, check_vma=False)
```

```python
import functools
import math

import jax
import jax.numpy as jnp
from jax import lax
from jax.experimental import pallas as pl
from jax.experimental.pallas import tpu as pltpu
from jax.sharding import PartitionSpec as P

MESH = pl.DeviceIdType.MESH
F32, BF16 = jnp.float32, jnp.bfloat16
NLAT = 1536
HALF = NLAT // 2
DEGREES = 1024
PAIRS = DEGREES // 2
SHELLS = 2048
SHELLS_DEV = 16
CHIP = 2 * SHELLS_DEV
FIELDS = 3
TILE = (8, 128)
CENTRAL_TERMS = [math.comb(2 * k, k) / 4.0**k for k in range(16)]


def central_ratio(counts):
    number = counts.astype(F32)
    bigger = jnp.maximum(number, 1.0)
    inverse = 1.0 / bigger
    series = 1.0 + inverse * (
        -0.125 + inverse * (0.0078125 + inverse * (0.0048828125 - inverse * 0.000640869140625))
    )
    result = series * lax.rsqrt(math.pi * bigger)
    for k in range(16):
        result = jnp.where(counts == k, CENTRAL_TERMS[k], result)
    return jnp.where(counts < 0, 0.0, result)


def cosine(phase):
    turn = 4.0 * NLAT
    number = phase.astype(F32)
    number = number - turn * jnp.floor(number * (1.0 / turn) + 0.5)
    angle = (NLAT - jnp.abs(number)) * (math.pi / (2 * NLAT))
    square = angle * angle
    total = jnp.full_like(square, 1.0 / math.factorial(13))
    for order in (11, 9, 7, 5, 3, 1):
        sign = -1.0 if order % 4 == 3 else 1.0
        total = sign / math.factorial(order) + square * total
    return angle * total


def split2(value):
    high = value.astype(BF16)
    low = (value - high.astype(F32)).astype(BF16)
    return high, low


def dot(left, right, transposed=False):
    dims = (((1,), (1 if transposed else 0,)), ((), ()))
    return lax.dot_general(left, right, dims, preferred_element_type=F32)


def dot3(left, high, low, transposed=False):
    rows = left.shape[0]
    top, rest = split2(left)
    both = dot(jnp.concatenate([top, rest], axis=0), high, transposed)
    return both[:rows] + both[rows:] + dot(top, low, transposed)


def permute_lanes(value, matrix):
    rows = value.shape[0]
    first = value.astype(BF16)
    left = value - first.astype(F32)
    second = left.astype(BF16)
    third = (left - second.astype(F32)).astype(BF16)
    out = dot(jnp.concatenate([first, second, third], axis=0), matrix)
    return out[:rows] + out[rows : 2 * rows] + out[2 * rows :]


def iota(shape, axis):
    return lax.broadcasted_iota(jnp.int32, shape, axis)


def level_parts(ports, own):
    count = len(ports)
    one, nothing = jnp.ones(TILE, F32), jnp.zeros(TILE, F32)

    def pick(place, new, old):
        return jnp.where(own == place, new, old)

    forward, backward = [None] * count, [None] * count
    a1, b1 = one, nothing
    pre_a1, pre_b1, thru_a1, thru_b1 = one, nothing, one, nothing
    for k in range(count):
        pa0, pb0, pa1, pb1 = ports[k]
        pre_a1, pre_b1 = pick(k, a1, pre_a1), pick(k, b1, pre_b1)
        beta = pa1 / (1.0 - b1 * pa0)
        forward[k] = (beta, beta * b1)
        a1, b1 = beta * a1, pb1 + beta * b1 * pb0
        thru_a1, thru_b1 = pick(k, a1, thru_a1), pick(k, b1, thru_b1)
    a0, b0 = nothing, one
    post_a0, post_b0, from_a0, from_b0 = nothing, one, nothing, one
    for k in reversed(range(count)):
        pa0, pb0, pa1, pb1 = ports[k]
        post_a0, post_b0 = pick(k, a0, post_a0), pick(k, b0, post_b0)
        gamma = pb0 / (1.0 - pb1 * a0)
        backward[k] = (gamma, gamma * a0)
        a0, b0 = pa0 + gamma * a0 * pa1, gamma * b0
        from_a0, from_b0 = pick(k, a0, from_a0), pick(k, b0, from_b0)
    lower_scale = 1.0 / (1.0 - pre_b1 * from_a0)
    upper_scale = 1.0 / (1.0 - post_a0 * thru_b1)
    lower = (lower_scale * pre_a1, lower_scale * pre_b1 * from_b0, lower_scale * pre_b1, lower_scale)
    upper = (
        upper_scale * post_a0 * thru_a1,
        upper_scale * post_b0,
        upper_scale * post_a0,
        upper_scale,
    )
    return forward, backward, lower, upper, (a0, b0, a1, b1)


def level_constants(parts, constants, own):
    forward, backward, lower, upper, _ = parts
    count = len(forward)
    nothing = jnp.zeros(TILE, F32)

    def pick(place, new, old):
        return jnp.where(own == place, new, old)

    c1, pre, thru = nothing, nothing, nothing
    for k in range(count):
        k0, k1 = constants[k]
        pre = pick(k, c1, pre)
        beta, beta_b = forward[k]
        c1 = (k1 + beta_b * k0) + beta * c1
        thru = pick(k, c1, thru)
    c0, post, start = nothing, nothing, nothing
    for k in reversed(range(count)):
        k0, k1 = constants[k]
        post = pick(k, c0, post)
        gamma, gamma_a = backward[k]
        c0 = (k0 + gamma_a * k1) + gamma * c0
        start = pick(k, c0, start)
    return c0, c1, lower[2] * start + lower[3] * pre, upper[2] * thru + upper[3] * post


def kernel(
    state_hbm,
    previous_hbm,
    below_hbm,
    above_hbm,
    kappa_hbm,
    new_ref,
    nonlinear_ref,
    state_raw,
    previous_raw,
    sides_raw,
    kappa_ref,
    mix,
    wide,
    tri_x,
    sent_x,
    got_x,
    forcing,
    ports_t,
    ports_h,
    exp_high,
    exp_low,
    angle_cos,
    angle_sin,
    cos_high,
    cos_low,
    sent_n,
    got_n,
    radial,
    green,
    solved,
    port_z,
    port_y,
    const_z,
    const_y,
    load_sem,
    x_send,
    x_recv,
    n_send,
    n_recv,
    u_send,
    u_recv,
    pz_send,
    pz_recv,
    py_send,
    py_recv,
    cz_send,
    cz_recv,
    cy_send,
    cy_recv,
):
    row, mode = lax.axis_index("row"), lax.axis_index("lm")
    y, z, core = row // 16, lax.rem(row // 2, 8), lax.rem(row, 2)
    other = row + 1 - 2 * core
    turn = [lax.rem(mode + d, 4) for d in range(4)]
    x_peers = [(row, turn[d]) for d in range(1, 4)]
    core_peers = [(other, turn[d]) for d in range(4)]
    z_peers = [(y * 16 + lax.rem(z + d, 8) * 2 + core, mode) for d in (4, 3, 5, 2, 6, 1, 7)]
    y_peers = [(lax.rem(y + d, 8) * 16 + z * 2 + core, mode) for d in (4, 3, 5, 2, 6, 1, 7)]

    barrier = pltpu.get_barrier_semaphore()
    everyone = z_peers + y_peers + x_peers + core_peers
    for peer in everyone:
        pl.semaphore_signal(barrier, inc=1, device_id=peer, device_id_type=MESH)

    loads = [
        pltpu.make_async_copy(state_hbm, state_raw, load_sem.at[0]),
        pltpu.make_async_copy(previous_hbm, previous_raw, load_sem.at[1]),
        pltpu.make_async_copy(below_hbm, sides_raw.at[0], load_sem.at[2]),
        pltpu.make_async_copy(above_hbm, sides_raw.at[1], load_sem.at[3]),
        pltpu.make_async_copy(kappa_hbm, kappa_ref, load_sem.at[4]),
    ]
    for load in loads:
        load.start()

    def send(source, target, send_sem, recv_sem, peer):
        copy = pltpu.make_async_remote_copy(
            src_ref=source,
            dst_ref=target,
            send_sem=send_sem,
            recv_sem=recv_sem,
            device_id=peer,
            device_id_type=MESH,
        )
        copy.start()
        return copy

    def receive(copies):
        for copy in copies:
            copy.wait_recv()

    source_id, target_id = iota((256, 256), 0), iota((256, 256), 1)
    part = (source_id == 2 * (target_id & 127) + (target_id >> 7)).astype(F32).astype(BF16)
    unite = (target_id == 2 * (source_id & 127) + (source_id >> 7)).astype(F32).astype(BF16)
    sub, lane = iota(TILE, 0), iota(TILE, 1)
    parity, field = sub >> 2, sub & 3
    degree = (mode * 256 + 2 * lane + parity).astype(F32)
    scale = jnp.sqrt(degree + 0.5)

    def to_tiles(values, target):
        for f in range(FIELDS):
            for p in range(2):
                target[pl.ds(p * 4 + f, SHELLS_DEV, stride=8), :] = values[
                    f * 16 : (f + 1) * 16, p * 128 : (p + 1) * 128
                ]

    def from_tiles(source):
        return jnp.concatenate(
            [
                jnp.concatenate(
                    [source[pl.ds(p * 4 + f, SHELLS_DEV, stride=8), :] for p in range(2)], axis=1
                )
                for f in range(FIELDS)
            ],
            axis=0,
        )

    tri_x[...] = jnp.zeros_like(tri_x)
    wide[...] = jnp.zeros_like(wide)
    loads[0].wait()
    to_tiles(permute_lanes(state_raw[...].reshape(48, 256), part), tri_x)
    sent_x[...] = tri_x[...].reshape(SHELLS_DEV, 8, 128) * scale
    pl.semaphore_wait(barrier, len(everyone))
    copies_x = [
        send(
            sent_x.at[pl.ds(peer[1] * 4, 4)],
            got_x.at[mode],
            x_send.at[d],
            x_recv.at[d],
            peer,
        )
        for d, peer in enumerate(x_peers)
    ]
    got_x[mode] = sent_x[pl.ds(mode * 4, 4)]

    loads[1].wait()
    to_tiles(permute_lanes(previous_raw[...].reshape(48, 256), part), wide)
    push = 4.0 * SHELLS_DEV * SHELLS_DEV
    forcing[pl.ds(core * SHELLS_DEV, SHELLS_DEV)] = (
        2.0 * tri_x[...] - (0.5 * push) * wide[...]
    ).reshape(SHELLS_DEV, 8, 128)
    copy_u = send(
        forcing.at[pl.ds(core * SHELLS_DEV, SHELLS_DEV)],
        forcing.at[pl.ds(core * SHELLS_DEV, SHELLS_DEV)],
        u_send.at[0],
        u_recv.at[0],
        core_peers[0],
    )

    toeplitz = central_ratio(512 + iota((8, 640), 0) - iota((8, 640), 1))
    hankel = [central_ratio(iota((8, 1024), 0) + iota((8, 1024), 1) + p) for p in range(2)]
    for step in range(16):
        rows = slice(step * 8, step * 8 + 8)
        moved = toeplitz if step == 0 else pltpu.roll(toeplitz, step * 8, 1)
        for b in range(4):
            ports_t[b, rows, :] = moved[:, (4 - b) * 128 : (5 - b) * 128]
        for p in range(2):
            moved = hankel[p] if step == 0 else pltpu.roll(hankel[p], 1024 - step * 8, 1)
            for b in range(7):
                ports_h[p, b, rows, :] = moved[:, b * 128 : (b + 1) * 128]
    for p in range(2):
        for a in range(4):
            for b in range(4):
                here = (p, slice(a * 128, a * 128 + 128), slice(b * 128, b * 128 + 128))
                if b <= a:
                    high, low = split2(ports_t[a - b] * ports_h[p, a + b])
                else:
                    high = low = jnp.zeros((128, 128), BF16)
                exp_high[here] = high
                exp_low[here] = low

    def phase(order, shape):
        return order * (2 * iota(shape, 1) + 1)

    wide_shape = (8, HALF)
    for p, groups in ((0, 7), (1, 4)):
        for group in range(groups):
            turns = phase(32 * (group * 8 + iota(wide_shape, 0)) + p, wide_shape)
            angle_cos[p, group * 8 : group * 8 + 8, :] = 2.0 * cosine(turns)
            angle_sin[p, group * 8 : group * 8 + 8, :] = 2.0 * cosine(turns - NLAT)
    base_shape = (16, HALF)
    turns = phase(2 * iota(base_shape, 0), base_shape)
    base_cos, base_sin = cosine(turns), cosine(turns - NLAT)
    base_row = iota((16, 128), 0)

    def series_term(q):
        order = (16 * q + base_row).astype(F32)
        term = -1.0 / (4.0 * order * order - 1.0)
        term = jnp.where(order > HALF, 0.0, term)
        return jnp.concatenate([term] * (HALF // 128), axis=1)

    def table_rows(p, q):
        return (
            angle_cos[p, pl.ds(q, 1), :] * base_cos - angle_sin[p, pl.ds(q, 1), :] * base_sin
        )

    def fill(q, weight):
        for p in range(2):
            values = table_rows(p, q)
            if p == 0:
                values = jnp.where((iota(base_shape, 0) + 16 * q) == 0, 1.0, values)
                weight = weight + series_term(q) * values
            high, low = split2(values)
            where = pl.ds(pl.multiple_of(q * 16, 16), 16)
            cos_high[p, where, :] = high
            cos_low[p, where, :] = low
        return weight

    weight = lax.fori_loop(0, 32, fill, jnp.zeros(base_shape, F32))
    weight = lax.fori_loop(
        32, 49, lambda q, weight: weight + series_term(q) * table_rows(0, q), weight
    )
    weight = jnp.sum(weight, axis=0, keepdims=True) * (2.0 / NLAT / 16.0)

    receive(copies_x)
    even_rows = (iota((32, 1), 0) & 4) == 0
    field_rows = iota((32, 1), 0) & 3
    sign = jnp.where(even_rows, 1.0, -1.0)

    def parities(left, right):
        return jnp.where(even_rows, left, right)

    def swap(values):
        return pltpu.roll(values.reshape(4, 8, values.shape[1]), 4, 1).reshape(values.shape)

    def rolled(values, shift):
        return pltpu.roll(values.reshape(4, 8, values.shape[1]), shift, 1).reshape(values.shape)

    spectrum = jnp.concatenate([got_x[k].reshape(32, 128) for k in range(4)], axis=1)
    half = PAIRS // 2

    def expand(p):
        first = dot3(spectrum, exp_high[p, :, :half], exp_low[p, :, :half])
        second = dot3(spectrum[:, half:], exp_high[p, half:, half:], exp_low[p, half:, half:])
        return jnp.concatenate([first, second], axis=1)

    orders = parities(expand(0), expand(1))
    sides = parities(*[dot3(orders, cos_high[p], cos_low[p]) for p in range(2)])
    grid = swap(sides) + sign * sides
    after, before, twice = rolled(grid, 7), rolled(grid, 1), rolled(grid, 2)
    product = jnp.where(
        field_rows == 0,
        after * after - grid * grid,
        jnp.where(field_rows == 1, before * grid, jnp.where(field_rows == 2, -(twice * grid), 0.0)),
    )
    product = product * weight
    folded = swap(product) + sign * product
    orders = parities(*[dot3(folded, cos_high[p], cos_low[p], True) for p in range(2)])

    def contract(p):
        first = dot3(orders[:, :half], exp_high[p, :half, :half], exp_low[p, :half, :half], True)
        second = dot3(orders, exp_high[p, half:, :], exp_low[p, half:, :], True)
        return jnp.concatenate([first, second], axis=1)

    terms = parities(contract(0), contract(1))
    for k in range(4):
        sent_n[k] = terms[:, k * 128 : (k + 1) * 128].reshape(4, 8, 128)
    mine = core * 4 + mode
    copies_n = [
        send(sent_n.at[peer[1]], got_n.at[mine], n_send.at[d], n_recv.at[d], peer)
        for d, peer in enumerate(x_peers + core_peers)
    ]
    got_n[mine] = sent_n[mode]

    loads[4].wait()
    kappa = jnp.full(TILE, 1.0, F32)
    for f in range(FIELDS):
        kappa = jnp.where(field == f, kappa_ref[f], kappa)
    spread = kappa * (16.0 * SHELLS_DEV * SHELLS_DEV)
    damping = kappa * (degree * (degree + 1.0)) * (1.0 / 256.0)
    first_shell = (row // 2) * CHIP
    for s in range(CHIP):
        number = jnp.full(TILE, (first_shell + s).astype(F32), F32)
        inverse = 1.0 / (0.5 + (number + 0.5) / (2.0 * SHELLS))
        slope = spread * (inverse * (1.0 / (2.0 * SHELLS)))
        radial[0, s] = (1.0 + 2.0 * spread) + damping * inverse * inverse
        radial[1, s] = spread - slope
        radial[2, s] = spread + slope
    cp, cq = jnp.zeros(TILE, F32), jnp.zeros(TILE, F32)
    for s in range(CHIP):
        t = CHIP - 1 - s
        ip = 1.0 / (radial[0, s] - radial[1, s] * cp)
        cp = radial[2, s] * ip
        radial[3, s], radial[4, s] = cp, ip
        iq = 1.0 / (radial[0, t] - radial[2, t] * cq)
        cq = radial[1, t] * iq
        radial[5, t], radial[6, t] = cq, iq
    low_run = up_run = head_run = tail_run = jnp.ones(TILE, F32)
    for s in range(CHIP):
        t = CHIP - 1 - s
        iq, ip = radial[6, s], radial[4, t]
        green[0, s] = iq * head_run
        head_run = head_run * (radial[2, s] * iq)
        low_run = low_run * radial[5, s]
        green[2, s] = low_run
        green[1, t] = ip * tail_run
        tail_run = tail_run * (radial[1, t] * ip)
        up_run = up_run * radial[3, t]
        green[3, t] = up_run
    port_z[z, 0], port_z[z, 1] = green[2, 0], green[3, 0]
    port_z[z, 2], port_z[z, 3] = green[2, CHIP - 1], green[3, CHIP - 1]
    copies_pz = [
        send(port_z.at[z], port_z.at[z], pz_send.at[d], pz_recv.at[d], peer)
        for d, peer in enumerate(z_peers)
    ]

    loads[2].wait()
    loads[3].wait()
    mix[...] = jnp.zeros_like(mix)
    for k in range(2):
        mix[k * 8 : k * 8 + FIELDS, :] = sides_raw[k, :, 0] + sides_raw[k, :, 1]
    parted = permute_lanes(mix[...], part)
    bottom, top = [
        jnp.concatenate([parted[k * 8 : k * 8 + 4, :128], parted[k * 8 : k * 8 + 4, 128:]], axis=0)
        for k in range(2)
    ]

    receive([copy_u])
    receive(copies_n)
    factor = (1.5 * push) * scale
    sums = [[None] * 4, [None] * 4]
    for s in range(CHIP):
        value = forcing[s] + factor * got_n[s // 4, s % 4]
        solved[s] = value
        for k in range(2):
            term = green[k, s] * value
            old = sums[k][s % 4]
            sums[k][s % 4] = term if old is None else old + term
    for k in range(2):
        const_z[z, k] = (sums[k][0] + sums[k][1]) + (sums[k][2] + sums[k][3])
    copies_cz = [
        send(const_z.at[z], const_z.at[z], cz_send.at[d], cz_recv.at[d], peer)
        for d, peer in enumerate(z_peers)
    ]

    receive(copies_pz)
    parts_z = level_parts([tuple(port_z[k, m] for m in range(4)) for k in range(8)], z)
    for m in range(4):
        port_y[y, m] = parts_z[4][m]
    copies_py = [
        send(port_y.at[y], port_y.at[y], py_send.at[d], py_recv.at[d], peer)
        for d, peer in enumerate(y_peers)
    ]

    run = jnp.zeros(TILE, F32)
    for s in range(CHIP):
        ip = radial[4, s]
        run = solved[s] * ip + (radial[1, s] * ip) * run
        solved[s] = run
    run = jnp.zeros(TILE, F32)
    for s in reversed(range(CHIP)):
        run = solved[s] + radial[3, s] * run
        solved[s] = run
    for q in range(4):
        wide[q * 32 : (q + 1) * 32, :] = (got_n[core * 4 + q] * scale).reshape(32, 128)
    nonlinear_ref[...] = permute_lanes(from_tiles(wide), unite).reshape(FIELDS, SHELLS_DEV, 256)

    receive(copies_cz)
    total0, total1, lower_z, upper_z = level_constants(
        parts_z, [(const_z[k, 0], const_z[k, 1]) for k in range(8)], z
    )
    const_y[y, 0], const_y[y, 1] = total0, total1
    copies_cy = [
        send(const_y.at[y], const_y.at[y], cy_send.at[d], cy_recv.at[d], peer)
        for d, peer in enumerate(y_peers)
    ]

    receive(copies_py)
    parts_y = level_parts([tuple(port_y[k, m] for m in range(4)) for k in range(8)], y)
    own_shells = pl.ds(core * SHELLS_DEV, SHELLS_DEV)
    rest = solved[own_shells] - tri_x[...].reshape(SHELLS_DEV, 8, 128)
    from_low, from_up = green[2, own_shells], green[3, own_shells]

    receive(copies_cy)
    _, _, lower_y, upper_y = level_constants(
        parts_y, [(const_y[k, 0], const_y[k, 1]) for k in range(8)], y
    )
    line_low = parts_y[2][0] * bottom + parts_y[2][1] * top + lower_y
    line_up = parts_y[3][0] * bottom + parts_y[3][1] * top + upper_y
    chip_low = parts_z[2][0] * line_low + parts_z[2][1] * line_up + lower_z
    chip_up = parts_z[3][0] * line_low + parts_z[3][1] * line_up + upper_z
    wide[...] = (rest + from_low * chip_low + from_up * chip_up).reshape(128, 128)
    new_ref[...] = permute_lanes(from_tiles(wide), unite).reshape(FIELDS, SHELLS_DEV, 256)

    for copy in copies_x + copies_n + [copy_u] + copies_pz + copies_py + copies_cz + copies_cy:
        copy.wait_send()


def write_out(new_ref, nonlinear_ref, new_hbm, nonlinear_hbm, sem):
    copies = [
        pltpu.make_async_copy(new_ref, new_hbm, sem.at[0]),
        pltpu.make_async_copy(nonlinear_ref, nonlinear_hbm, sem.at[1]),
    ]
    for copy in copies:
        copy.start()
    for copy in copies:
        copy.wait()


def local(state, previous_terms, below, above, kappa):
    block = jax.ShapeDtypeStruct(state.shape, F32)
    vmem, dma = pltpu.VMEM, pltpu.SemaphoreType.DMA
    anywhere = pl.BlockSpec(memory_space=pl.ANY)
    inside = pl.BlockSpec(memory_space=pltpu.VMEM)
    scratch = [
        vmem((FIELDS, SHELLS_DEV, 256), F32),
        vmem((FIELDS, SHELLS_DEV, 256), F32),
        vmem((2, FIELDS, 2, 256), F32),
        pltpu.SMEM((FIELDS,), F32),
        vmem((16, 256), F32),
        vmem((128, 128), F32),
        vmem((128, 128), F32),
        vmem((16, 8, 128), F32),
        vmem((4, 4, 8, 128), F32),
        vmem((CHIP, 8, 128), F32),
        vmem((4, 128, 128), F32),
        vmem((2, 7, 128, 128), F32),
        vmem((2, PAIRS, PAIRS), BF16),
        vmem((2, PAIRS, PAIRS), BF16),
        vmem((2, 56, HALF), F32),
        vmem((2, 56, HALF), F32),
        vmem((2, PAIRS, HALF), BF16),
        vmem((2, PAIRS, HALF), BF16),
        vmem((4, 4, 8, 128), F32),
        vmem((8, 4, 8, 128), F32),
        vmem((7, CHIP, 8, 128), F32),
        vmem((4, CHIP, 8, 128), F32),
        vmem((CHIP, 8, 128), F32),
        vmem((8, 4, 8, 128), F32),
        vmem((8, 4, 8, 128), F32),
        vmem((8, 2, 8, 128), F32),
        vmem((8, 2, 8, 128), F32),
        dma((5,)),
        dma((3,)),
        dma((3,)),
        dma((7,)),
        dma((7,)),
        dma((1,)),
        dma((1,)),
    ] + [dma((7,))] * 8
    held = pltpu.VMEM(state.shape, F32)
    operands = [
        pltpu.with_memory_space_constraint(operand, pltpu.HBM)
        for operand in (
            state,
            previous_terms,
            jnp.transpose(below, (1, 0, 2)),
            jnp.transpose(above, (1, 0, 2)),
            kappa,
        )
    ]
    results = pl.pallas_call(
        kernel,
        out_shape=(held, held),
        in_specs=[anywhere] * 5,
        out_specs=(inside, inside),
        scratch_shapes=scratch,
        compiler_params=pltpu.CompilerParams(
            collective_id=0, has_side_effects=True, vmem_limit_bytes=32 * 1024 * 1024
        ),
    )(*operands)
    return pl.pallas_call(
        write_out,
        out_shape=(block, block),
        in_specs=[inside] * 2,
        out_specs=(anywhere, anywhere),
        scratch_shapes=[dma((2,))],
    )(*[pltpu.with_memory_space_constraint(result, pltpu.VMEM) for result in results])


def solution(mesh):
    in_specs = (
        P(None, "row", "lm"),
        P(None, "row", "lm"),
        P(None, None, "lm"),
        P(None, None, "lm"),
        P(),
    )
    out_specs = (P(None, "row", "lm"), P(None, "row", "lm"))
    return jax.shard_map(local, mesh=mesh, in_specs=in_specs, out_specs=out_specs, check_vma=False)
```

```python
import functools
import math

import jax
import jax.numpy as jnp
from jax import lax
from jax.experimental import pallas as pl
from jax.experimental.pallas import tpu as pltpu
from jax.sharding import PartitionSpec as P

MESH = pl.DeviceIdType.MESH
F32, BF16 = jnp.float32, jnp.bfloat16
NLAT = 1536
HALF = NLAT // 2
DEGREES = 1024
PAIRS = DEGREES // 2
SHELLS = 2048
SHELLS_DEV = 16
CHIP = 2 * SHELLS_DEV
FIELDS = 3
TILE = (8, 128)
CENTRAL_TERMS = [math.comb(2 * k, k) / 4.0**k for k in range(16)]


def central_ratio(counts):
    number = counts.astype(F32)
    bigger = jnp.maximum(number, 1.0)
    inverse = 1.0 / bigger
    series = 1.0 + inverse * (
        -0.125 + inverse * (0.0078125 + inverse * (0.0048828125 - inverse * 0.000640869140625))
    )
    result = series / jnp.sqrt(math.pi * bigger)
    for k in range(16):
        result = jnp.where(counts == k, CENTRAL_TERMS[k], result)
    return jnp.where(counts < 0, 0.0, result)


def cosine(phase):
    turn = 4.0 * NLAT
    number = phase.astype(F32)
    number = number - turn * jnp.floor(number * (1.0 / turn) + 0.5)
    angle = (NLAT - jnp.abs(number)) * (math.pi / (2 * NLAT))
    square = angle * angle
    total = jnp.full_like(square, 1.0 / math.factorial(13))
    for order in (11, 9, 7, 5, 3, 1):
        sign = -1.0 if order % 4 == 3 else 1.0
        total = sign / math.factorial(order) + square * total
    return angle * total


def split2(value):
    high = value.astype(BF16)
    low = (value - high.astype(F32)).astype(BF16)
    return high, low


def dot(left, right, transposed=False):
    dims = (((1,), (1 if transposed else 0,)), ((), ()))
    return lax.dot_general(left, right, dims, preferred_element_type=F32)


def dot3(left, high, low, transposed=False):
    rows = left.shape[0]
    top, rest = split2(left)
    both = dot(jnp.concatenate([top, rest], axis=0), high, transposed)
    return both[:rows] + both[rows:] + dot(top, low, transposed)


def permute_lanes(value, matrix):
    rows = value.shape[0]
    first = value.astype(BF16)
    left = value - first.astype(F32)
    second = left.astype(BF16)
    third = (left - second.astype(F32)).astype(BF16)
    out = dot(jnp.concatenate([first, second, third], axis=0), matrix)
    return out[:rows] + out[rows : 2 * rows] + out[2 * rows :]


def iota(shape, axis):
    return lax.broadcasted_iota(jnp.int32, shape, axis)


def level_parts(ports, own):
    count = len(ports)
    one, nothing = jnp.ones(TILE, F32), jnp.zeros(TILE, F32)

    def pick(place, new, old):
        return jnp.where(own == place, new, old)

    forward, backward = [None] * count, [None] * count
    a1, b1 = one, nothing
    pre_a1, pre_b1, thru_a1, thru_b1 = one, nothing, one, nothing
    for k in range(count):
        pa0, pb0, pa1, pb1 = ports[k]
        pre_a1, pre_b1 = pick(k, a1, pre_a1), pick(k, b1, pre_b1)
        beta = pa1 / (1.0 - b1 * pa0)
        forward[k] = (beta, beta * b1)
        a1, b1 = beta * a1, pb1 + beta * b1 * pb0
        thru_a1, thru_b1 = pick(k, a1, thru_a1), pick(k, b1, thru_b1)
    a0, b0 = nothing, one
    post_a0, post_b0, from_a0, from_b0 = nothing, one, nothing, one
    for k in reversed(range(count)):
        pa0, pb0, pa1, pb1 = ports[k]
        post_a0, post_b0 = pick(k, a0, post_a0), pick(k, b0, post_b0)
        gamma = pb0 / (1.0 - pb1 * a0)
        backward[k] = (gamma, gamma * a0)
        a0, b0 = pa0 + gamma * a0 * pa1, gamma * b0
        from_a0, from_b0 = pick(k, a0, from_a0), pick(k, b0, from_b0)
    lower_scale = 1.0 / (1.0 - pre_b1 * from_a0)
    upper_scale = 1.0 / (1.0 - post_a0 * thru_b1)
    lower = (lower_scale * pre_a1, lower_scale * pre_b1 * from_b0, lower_scale * pre_b1, lower_scale)
    upper = (
        upper_scale * post_a0 * thru_a1,
        upper_scale * post_b0,
        upper_scale * post_a0,
        upper_scale,
    )
    return forward, backward, lower, upper, (a0, b0, a1, b1)


def level_constants(parts, constants, own):
    forward, backward, lower, upper, _ = parts
    count = len(forward)
    nothing = jnp.zeros(TILE, F32)

    def pick(place, new, old):
        return jnp.where(own == place, new, old)

    c1, pre, thru = nothing, nothing, nothing
    for k in range(count):
        k0, k1 = constants[k]
        pre = pick(k, c1, pre)
        beta, beta_b = forward[k]
        c1 = (k1 + beta_b * k0) + beta * c1
        thru = pick(k, c1, thru)
    c0, post, start = nothing, nothing, nothing
    for k in reversed(range(count)):
        k0, k1 = constants[k]
        post = pick(k, c0, post)
        gamma, gamma_a = backward[k]
        c0 = (k0 + gamma_a * k1) + gamma * c0
        start = pick(k, c0, start)
    return c0, c1, lower[2] * start + lower[3] * pre, upper[2] * thru + upper[3] * post


def kernel(
    state_hbm,
    previous_hbm,
    below_hbm,
    above_hbm,
    kappa_hbm,
    new_ref,
    nonlinear_ref,
    state_raw,
    previous_raw,
    sides_raw,
    kappa_ref,
    mix,
    wide,
    tri_x,
    sent_x,
    got_x,
    forcing,
    ports_t,
    ports_h,
    exp_high,
    exp_low,
    angle_cos,
    angle_sin,
    cos_high,
    cos_low,
    flip_high,
    flip_low,
    sent_n,
    got_n,
    shell_q,
    partial,
    green,
    solved,
    port_y,
    const_z,
    const_y,
    relay_sem,
    load_sem,
    x_send,
    x_recv,
    n_send,
    n_recv,
    u_send,
    u_recv,
    py_send,
    py_recv,
    cz_send,
    cz_recv,
    cy_send,
    cy_recv,
):
    row, mode = lax.axis_index("row"), lax.axis_index("lm")
    y, z, core = row // 16, lax.rem(row // 2, 8), lax.rem(row, 2)
    other = row + 1 - 2 * core
    turn = [lax.rem(mode + d, 4) for d in range(4)]
    x_peers = [(row, turn[d]) for d in range(1, 4)]
    core_peers = [(other, turn[d]) for d in range(4)]

    loads = [
        pltpu.make_async_copy(state_hbm, state_raw, load_sem.at[0]),
        pltpu.make_async_copy(previous_hbm, previous_raw, load_sem.at[1]),
        pltpu.make_async_copy(below_hbm, sides_raw.at[0], load_sem.at[2]),
        pltpu.make_async_copy(above_hbm, sides_raw.at[1], load_sem.at[3]),
        pltpu.make_async_copy(kappa_hbm, kappa_ref, load_sem.at[4]),
    ]
    for load in loads:
        load.start()

    def along_z(d):
        return (y * 16 + lax.rem(z + d, 8) * 2 + core, mode)

    def along_y(d):
        return (lax.rem(y + d, 8) * 16 + z * 2 + core, mode)

    z_peers = [along_z(d) for d in (4, 3, 5, 2, 6, 1, 7)]
    y_peers = [along_y(d) for d in (4, 3, 5, 2, 6, 1, 7)]

    barrier = pltpu.get_barrier_semaphore()
    near = x_peers + core_peers + [line(d) for line in (along_z, along_y) for d in (1, 7)]
    for peer in near:
        pl.semaphore_signal(barrier, inc=1, device_id=peer, device_id_type=MESH)

    def relay(step):
        for k, line in enumerate((along_z, along_y)):
            for side, d in enumerate((step, 8 - step)):
                pl.semaphore_signal(
                    relay_sem.at[step - 1, k, side],
                    inc=1,
                    device_id=line(d),
                    device_id_type=MESH,
                )

    def relayed(step):
        for k in range(2):
            for side in range(2):
                pl.semaphore_wait(relay_sem.at[step - 1, k, side], 1)

    def send(source, target, send_sem, recv_sem, peer):
        copy = pltpu.make_async_remote_copy(
            src_ref=source,
            dst_ref=target,
            send_sem=send_sem,
            recv_sem=recv_sem,
            device_id=peer,
            device_id_type=MESH,
        )
        copy.start()
        return copy

    def receive(copies):
        for copy in copies:
            copy.wait_recv()

    source_id, target_id = iota((256, 256), 0), iota((256, 256), 1)
    part = (source_id == 2 * (target_id & 127) + (target_id >> 7)).astype(F32).astype(BF16)
    unite = (target_id == 2 * (source_id & 127) + (source_id >> 7)).astype(F32).astype(BF16)
    sub, lane = iota(TILE, 0), iota(TILE, 1)
    parity, field = sub >> 2, sub & 3
    degree = (mode * 256 + 2 * lane + parity).astype(F32)
    scale = jnp.sqrt(degree + 0.5)

    def to_tiles(values, target):
        for f in range(FIELDS):
            for p in range(2):
                target[pl.ds(p * 4 + f, SHELLS_DEV, stride=8), :] = values[
                    f * 16 : (f + 1) * 16, p * 128 : (p + 1) * 128
                ]

    def from_tiles(source):
        return jnp.concatenate(
            [
                jnp.concatenate(
                    [source[pl.ds(p * 4 + f, SHELLS_DEV, stride=8), :] for p in range(2)], axis=1
                )
                for f in range(FIELDS)
            ],
            axis=0,
        )

    toeplitz = central_ratio(512 + iota((8, 640), 0) - iota((8, 640), 1))
    hankel = [central_ratio(iota((8, 1024), 0) + iota((8, 1024), 1) + p) for p in range(2)]
    for step in range(16):
        rows = slice(step * 8, step * 8 + 8)
        moved = toeplitz if step == 0 else pltpu.roll(toeplitz, step * 8, 1)
        for b in range(4):
            ports_t[b, rows, :] = moved[:, (4 - b) * 128 : (5 - b) * 128]
        for p in range(2):
            moved = hankel[p] if step == 0 else pltpu.roll(hankel[p], 1024 - step * 8, 1)
            for b in range(7):
                ports_h[p, b, rows, :] = moved[:, b * 128 : (b + 1) * 128]
    for p in range(2):
        for a in range(4):
            for b in range(4):
                here = (p, slice(a * 128, a * 128 + 128), slice(b * 128, b * 128 + 128))
                if b <= a:
                    high, low = split2(ports_t[a - b] * ports_h[p, a + b])
                else:
                    high = low = jnp.zeros((128, 128), BF16)
                exp_high[here] = high
                exp_low[here] = low

    tri_x[...] = jnp.zeros_like(tri_x)
    wide[...] = jnp.zeros_like(wide)
    loads[0].wait()
    to_tiles(permute_lanes(state_raw[...].reshape(48, 256), part), tri_x)
    sent_x[...] = tri_x[...].reshape(SHELLS_DEV, 8, 128) * scale
    pl.semaphore_wait(barrier, len(near))
    copies_x = [
        send(
            sent_x.at[pl.ds(peer[1] * 4, 4)],
            got_x.at[mode],
            x_send.at[d],
            x_recv.at[d],
            peer,
        )
        for d, peer in enumerate(x_peers)
    ]
    relay(1)
    got_x[mode] = sent_x[pl.ds(mode * 4, 4)]

    def phase(order, shape):
        return order * (2 * iota(shape, 1) + 1)

    wide_shape = (8, HALF)
    for p, groups in ((0, 7), (1, 4)):
        for group in range(groups):
            turns = phase(32 * (group * 8 + iota(wide_shape, 0)) + p, wide_shape)
            angle_cos[p, group * 8 : group * 8 + 8, :] = 2.0 * cosine(turns)
            angle_sin[p, group * 8 : group * 8 + 8, :] = 2.0 * cosine(turns - NLAT)
    base_shape = (16, HALF)
    turns = phase(2 * iota(base_shape, 0), base_shape)
    base_cos, base_sin = cosine(turns), cosine(turns - NLAT)
    base_row = iota((16, 128), 0)

    def series_term(q):
        order = (16 * q + base_row).astype(F32)
        term = -1.0 / (4.0 * order * order - 1.0)
        term = jnp.where(order > HALF, 0.0, term)
        return jnp.concatenate([term] * (HALF // 128), axis=1)

    def table_rows(p, q):
        return (
            angle_cos[p, pl.ds(q, 1), :] * base_cos - angle_sin[p, pl.ds(q, 1), :] * base_sin
        )

    def fill(q, weight):
        for p in range(2):
            values = table_rows(p, q)
            if p == 0:
                values = jnp.where((iota(base_shape, 0) + 16 * q) == 0, 1.0, values)
                weight = weight + series_term(q) * values
            high, low = split2(values)
            where = pl.ds(pl.multiple_of(q * 16, 16), 16)
            cos_high[p, where, :] = high
            cos_low[p, where, :] = low
        return weight

    weight = lax.fori_loop(0, 32, fill, jnp.zeros(base_shape, F32))
    weight = lax.fori_loop(
        32, 49, lambda q, weight: weight + series_term(q) * table_rows(0, q), weight
    )
    weight = jnp.sum(weight, axis=0, keepdims=True) * (2.0 / NLAT / 16.0)

    for p in range(2):
        for table, flipped in ((cos_high, flip_high), (cos_low, flip_low)):
            for block in range(0, PAIRS, 128):
                flipped[p, :, block : block + 128] = table[p, block : block + 128, :].T
    receive(copies_x)
    even_rows = (iota((32, 1), 0) & 4) == 0
    field_rows = iota((32, 1), 0) & 3
    sign = jnp.where(even_rows, 1.0, -1.0)

    def parities(left, right):
        return jnp.where(even_rows, left, right)

    def swap(values):
        return pltpu.roll(values.reshape(4, 8, values.shape[1]), 4, 1).reshape(values.shape)

    def rolled(values, shift):
        return pltpu.roll(values.reshape(4, 8, values.shape[1]), shift, 1).reshape(values.shape)

    spectrum = jnp.concatenate([got_x[k].reshape(32, 128) for k in range(4)], axis=1)
    half = PAIRS // 2

    def expand(p):
        first = dot3(spectrum, exp_high[p, :, :half], exp_low[p, :, :half])
        second = dot3(spectrum[:, half:], exp_high[p, half:, half:], exp_low[p, half:, half:])
        return jnp.concatenate([first, second], axis=1)

    orders = parities(expand(0), expand(1))
    sides = parities(*[dot3(orders, cos_high[p], cos_low[p]) for p in range(2)])
    grid = swap(sides) + sign * sides
    after, before, twice = rolled(grid, 7), rolled(grid, 1), rolled(grid, 2)
    product = jnp.where(
        field_rows == 0,
        after * after - grid * grid,
        jnp.where(field_rows == 1, before * grid, jnp.where(field_rows == 2, -(twice * grid), 0.0)),
    )
    product = product * weight
    folded = swap(product) + sign * product
    orders = parities(*[dot3(folded, flip_high[p], flip_low[p]) for p in range(2)])

    def contract(p):
        first = dot3(orders[:, :half], exp_high[p, :half, :half], exp_low[p, :half, :half], True)
        second = dot3(orders, exp_high[p, half:, :], exp_low[p, half:, :], True)
        return jnp.concatenate([first, second], axis=1)

    terms = parities(contract(0), contract(1))
    for k in range(4):
        sent_n[k] = terms[:, k * 128 : (k + 1) * 128].reshape(4, 8, 128)
    mine = core * 4 + mode
    copies_n = [
        send(sent_n.at[peer[1]], got_n.at[mine], n_send.at[d], n_recv.at[d], peer)
        for d, peer in enumerate(x_peers + core_peers)
    ]
    got_n[mine] = sent_n[mode]
    relayed(1)
    relay(2)

    loads[1].wait()
    to_tiles(permute_lanes(previous_raw[...].reshape(48, 256), part), wide)
    push = 4.0 * SHELLS_DEV * SHELLS_DEV
    forcing[pl.ds(core * SHELLS_DEV, SHELLS_DEV)] = (
        2.0 * tri_x[...] - (0.5 * push) * wide[...]
    ).reshape(SHELLS_DEV, 8, 128)
    copy_u = send(
        forcing.at[pl.ds(core * SHELLS_DEV, SHELLS_DEV)],
        forcing.at[pl.ds(core * SHELLS_DEV, SHELLS_DEV)],
        u_send.at[0],
        u_recv.at[0],
        core_peers[0],
    )

    loads[4].wait()
    kappa = jnp.full(TILE, 1.0, F32)
    for f in range(FIELDS):
        kappa = jnp.where(field == f, kappa_ref[f], kappa)
    alpha = 1.0 / (kappa * (16.0 * SHELLS_DEV * SHELLS_DEV))
    steep = 16.0 * (degree * (degree + 1.0))
    one = jnp.ones(TILE, F32)
    for block in range(SHELLS // 256):
        rho = (iota((256, 128), 0) + block * 256).astype(F32) + (SHELLS + 0.5)
        shell_q[block * 256 : (block + 1) * 256, :] = 1.0 / (rho * rho)

    def beta(shell):
        return alpha + steep * shell_q[pl.ds(shell, 1), :]

    first_shell = (row // 2) * CHIP
    grow, change = one, one
    back, back_change = one, one
    for s in range(CHIP):
        green[1, s] = grow
        change = beta(first_shell + s) * grow + change
        grow = grow + change
        t = CHIP - 1 - s
        green[0, t] = back
        back_change = beta(first_shell + t) * back + back_change
        back = back + back_change
    inverse = 1.0 / grow
    for s in range(CHIP):
        green[0, s] = green[0, s] * inverse
        green[1, s] = green[1, s] * inverse

    def line_ports(line):
        starts = [line * 256 + k * CHIP for k in range(8)]
        carry = []
        for start in starts:
            change = beta(start) + one
            carry += [one + change, change, one, one]

        def step(s, carry):
            after = []
            for k, start in enumerate(starts):
                grow, change, inner, inner_change = carry[4 * k : 4 * k + 4]
                here = beta(start + s)
                change = here * grow + change
                inner_change = here * inner + inner_change
                after += [grow + change, change, inner + inner_change, inner_change]
            return tuple(after)

        carry = lax.fori_loop(1, CHIP, step, tuple(carry))
        ports = []
        for k in range(8):
            grow, change, inner, _ = carry[4 * k : 4 * k + 4]
            tau = 1.0 / grow
            ports.append((inner * tau, tau, tau, (grow - change) * tau))
        return ports

    parts_z = level_parts(line_ports(y), z)
    port_y[y, 0], port_y[y, 1], port_y[y, 2] = parts_z[4][0], parts_z[4][1], parts_z[4][3]

    loads[2].wait()
    loads[3].wait()
    mix[...] = jnp.zeros_like(mix)
    for k in range(2):
        mix[k * 8 : k * 8 + FIELDS, :] = sides_raw[k, :, 0] + sides_raw[k, :, 1]
    parted = permute_lanes(mix[...], part)
    bottom, top = [
        jnp.concatenate([parted[k * 8 : k * 8 + 4, :128], parted[k * 8 : k * 8 + 4, 128:]], axis=0)
        for k in range(2)
    ]
    bottom, top = bottom * (SHELLS - 0.5), top * (2 * SHELLS + 0.5)

    relayed(2)
    copies_py = [
        send(port_y.at[y], port_y.at[y], py_send.at[d], py_recv.at[d], peer)
        for d, peer in enumerate(y_peers)
    ]

    receive([copy_u])
    receive(copies_n)
    factor = (1.5 * push) * scale
    sums = [[None] * 4, [None] * 4]
    for s in range(CHIP):
        rho = (first_shell + s).astype(F32) + (SHELLS + 0.5)
        value = (alpha * rho) * (forcing[s] + factor * got_n[s // 4, s % 4])
        solved[s] = value
        for k in range(2):
            term = green[k, s] * value
            old = sums[k][s % 4]
            sums[k][s % 4] = term if old is None else old + term
    for k in range(2):
        const_z[z, k] = (sums[k][0] + sums[k][1]) + (sums[k][2] + sums[k][3])
    copies_cz = [
        send(const_z.at[z], const_z.at[z], cz_send.at[d], cz_recv.at[d], peer)
        for d, peer in enumerate(z_peers)
    ]

    run = jnp.zeros(TILE, F32)
    for s in range(CHIP):
        run = run + (green[1, s] * grow) * solved[s]
        partial[s] = green[0, s] * run
    run = jnp.zeros(TILE, F32)
    for s in reversed(range(CHIP)):
        solved_here = solved[s]
        solved[s] = partial[s] + green[1, s] * run
        run = run + (green[0, s] * grow) * solved_here

    for q in range(4):
        wide[q * 32 : (q + 1) * 32, :] = (got_n[core * 4 + q] * scale).reshape(32, 128)
    nonlinear_ref[...] = permute_lanes(from_tiles(wide), unite).reshape(FIELDS, SHELLS_DEV, 256)

    receive(copies_cz)
    total0, total1, lower_z, upper_z = level_constants(
        parts_z, [(const_z[k, 0], const_z[k, 1]) for k in range(8)], z
    )
    const_y[y, 0], const_y[y, 1] = total0, total1
    copies_cy = [
        send(const_y.at[y], const_y.at[y], cy_send.at[d], cy_recv.at[d], peer)
        for d, peer in enumerate(y_peers)
    ]

    own_shells = pl.ds(core * SHELLS_DEV, SHELLS_DEV)
    number = (row * SHELLS_DEV + iota((SHELLS_DEV, 8, 128), 0)).astype(F32) + (SHELLS + 0.5)
    over = 1.0 / number
    rest = solved[own_shells] * over - tri_x[...].reshape(SHELLS_DEV, 8, 128)
    from_low, from_up = green[0, own_shells] * over, green[1, own_shells] * over

    receive(copies_py)
    parts_y = level_parts(
        [(port_y[k, 0], port_y[k, 1], port_y[k, 1], port_y[k, 2]) for k in range(8)], y
    )
    receive(copies_cy)
    _, _, lower_y, upper_y = level_constants(
        parts_y, [(const_y[k, 0], const_y[k, 1]) for k in range(8)], y
    )
    line_low = parts_y[2][0] * bottom + parts_y[2][1] * top + lower_y
    line_up = parts_y[3][0] * bottom + parts_y[3][1] * top + upper_y
    chip_low = parts_z[2][0] * line_low + parts_z[2][1] * line_up + lower_z
    chip_up = parts_z[3][0] * line_low + parts_z[3][1] * line_up + upper_z
    wide[...] = (rest + from_low * chip_low + from_up * chip_up).reshape(128, 128)
    new_ref[...] = permute_lanes(from_tiles(wide), unite).reshape(FIELDS, SHELLS_DEV, 256)

    for copy in copies_x + copies_n + [copy_u] + copies_py + copies_cz + copies_cy:
        copy.wait_send()


def write_out(new_ref, nonlinear_ref, new_hbm, nonlinear_hbm, sem):
    copies = [
        pltpu.make_async_copy(new_ref, new_hbm, sem.at[0]),
        pltpu.make_async_copy(nonlinear_ref, nonlinear_hbm, sem.at[1]),
    ]
    for copy in copies:
        copy.start()
    for copy in copies:
        copy.wait()


def local(state, previous_terms, below, above, kappa):
    block = jax.ShapeDtypeStruct(state.shape, F32)
    vmem, dma = pltpu.VMEM, pltpu.SemaphoreType.DMA
    anywhere = pl.BlockSpec(memory_space=pl.ANY)
    inside = pl.BlockSpec(memory_space=pltpu.VMEM)
    scratch = [
        vmem((FIELDS, SHELLS_DEV, 256), F32),
        vmem((FIELDS, SHELLS_DEV, 256), F32),
        vmem((2, FIELDS, 2, 256), F32),
        pltpu.SMEM((FIELDS,), F32),
        vmem((16, 256), F32),
        vmem((128, 128), F32),
        vmem((128, 128), F32),
        vmem((16, 8, 128), F32),
        vmem((4, 4, 8, 128), F32),
        vmem((CHIP, 8, 128), F32),
        vmem((4, 128, 128), F32),
        vmem((2, 7, 128, 128), F32),
        vmem((2, PAIRS, PAIRS), BF16),
        vmem((2, PAIRS, PAIRS), BF16),
        vmem((2, 56, HALF), F32),
        vmem((2, 56, HALF), F32),
        vmem((2, PAIRS, HALF), BF16),
        vmem((2, PAIRS, HALF), BF16),
        vmem((2, HALF, PAIRS), BF16),
        vmem((2, HALF, PAIRS), BF16),
        vmem((4, 4, 8, 128), F32),
        vmem((8, 4, 8, 128), F32),
        vmem((SHELLS, 128), F32),
        vmem((CHIP, 8, 128), F32),
        vmem((2, CHIP, 8, 128), F32),
        vmem((CHIP, 8, 128), F32),
        vmem((8, 3, 8, 128), F32),
        vmem((8, 2, 8, 128), F32),
        vmem((8, 2, 8, 128), F32),
        pltpu.SemaphoreType.REGULAR((2, 2, 2)),
        dma((5,)),
        dma((3,)),
        dma((3,)),
        dma((7,)),
        dma((7,)),
        dma((1,)),
        dma((1,)),
    ] + [dma((7,))] * 6
    held = pltpu.VMEM(state.shape, F32)
    operands = [
        pltpu.with_memory_space_constraint(operand, pltpu.HBM)
        for operand in (
            state,
            previous_terms,
            jnp.transpose(below, (1, 0, 2)),
            jnp.transpose(above, (1, 0, 2)),
            kappa,
        )
    ]
    results = pl.pallas_call(
        kernel,
        out_shape=(held, held),
        in_specs=[anywhere] * 5,
        out_specs=(inside, inside),
        scratch_shapes=scratch,
        compiler_params=pltpu.CompilerParams(
            collective_id=0, has_side_effects=True, vmem_limit_bytes=32 * 1024 * 1024
        ),
    )(*operands)
    return pl.pallas_call(
        write_out,
        out_shape=(block, block),
        in_specs=[inside] * 2,
        out_specs=(anywhere, anywhere),
        scratch_shapes=[dma((2,))],
    )(*[pltpu.with_memory_space_constraint(result, pltpu.VMEM) for result in results])


def solution(mesh):
    in_specs = (
        P(None, "row", "lm"),
        P(None, "row", "lm"),
        P(None, None, "lm"),
        P(None, None, "lm"),
        P(),
    )
    out_specs = (P(None, "row", "lm"), P(None, "row", "lm"))
    return jax.shard_map(local, mesh=mesh, in_specs=in_specs, out_specs=out_specs, check_vma=False)
```

```python
import functools
import math

import jax
import jax.numpy as jnp
from jax import lax
from jax.experimental import pallas as pl
from jax.experimental.pallas import tpu as pltpu
from jax.sharding import PartitionSpec as P

MESH = pl.DeviceIdType.MESH
F32, BF16 = jnp.float32, jnp.bfloat16
NLAT = 1536
HALF = NLAT // 2
DEGREES = 1024
PAIRS = DEGREES // 2
SHELLS = 2048
SHELLS_DEV = 16
CHIP = 2 * SHELLS_DEV
FIELDS = 3
TILE = (8, 128)
CENTRAL_TERMS = [math.comb(2 * k, k) / 4.0**k for k in range(16)]


def central_ratio(counts):
    number = counts.astype(F32)
    bigger = jnp.maximum(number, 1.0)
    inverse = 1.0 / bigger
    series = 1.0 + inverse * (
        -0.125 + inverse * (0.0078125 + inverse * (0.0048828125 - inverse * 0.000640869140625))
    )
    result = series / jnp.sqrt(math.pi * bigger)
    for k in range(16):
        result = jnp.where(counts == k, CENTRAL_TERMS[k], result)
    return jnp.where(counts < 0, 0.0, result)


def cosine(phase):
    turn = 4.0 * NLAT
    number = phase.astype(F32)
    number = number - turn * jnp.floor(number * (1.0 / turn) + 0.5)
    angle = (NLAT - jnp.abs(number)) * (math.pi / (2 * NLAT))
    square = angle * angle
    total = jnp.full_like(square, 1.0 / math.factorial(13))
    for order in (11, 9, 7, 5, 3, 1):
        sign = -1.0 if order % 4 == 3 else 1.0
        total = sign / math.factorial(order) + square * total
    return angle * total


def split2(value):
    high = value.astype(BF16)
    low = (value - high.astype(F32)).astype(BF16)
    return high, low


def dot(left, right, transposed=False):
    dims = (((1,), (1 if transposed else 0,)), ((), ()))
    return lax.dot_general(left, right, dims, preferred_element_type=F32)


def dot3(left, high, low, transposed=False):
    rows = left.shape[0]
    top, rest = split2(left)
    both = dot(jnp.concatenate([top, rest], axis=0), high, transposed)
    return both[:rows] + both[rows:] + dot(top, low, transposed)


def permute_lanes(value, matrix):
    rows = value.shape[0]
    first = value.astype(BF16)
    left = value - first.astype(F32)
    second = left.astype(BF16)
    third = (left - second.astype(F32)).astype(BF16)
    out = dot(jnp.concatenate([first, second, third], axis=0), matrix)
    return out[:rows] + out[rows : 2 * rows] + out[2 * rows :]


def iota(shape, axis):
    return lax.broadcasted_iota(jnp.int32, shape, axis)


def level_parts(ports, own):
    count = len(ports)
    one, nothing = jnp.ones(TILE, F32), jnp.zeros(TILE, F32)

    def pick(place, new, old):
        return jnp.where(own == place, new, old)

    forward, backward = [None] * count, [None] * count
    a1, b1 = one, nothing
    pre_a1, pre_b1, thru_a1, thru_b1 = one, nothing, one, nothing
    for k in range(count):
        pa0, pb0, pa1, pb1 = ports[k]
        pre_a1, pre_b1 = pick(k, a1, pre_a1), pick(k, b1, pre_b1)
        beta = pa1 / (1.0 - b1 * pa0)
        forward[k] = (beta, beta * b1)
        a1, b1 = beta * a1, pb1 + beta * b1 * pb0
        thru_a1, thru_b1 = pick(k, a1, thru_a1), pick(k, b1, thru_b1)
    a0, b0 = nothing, one
    post_a0, post_b0, from_a0, from_b0 = nothing, one, nothing, one
    for k in reversed(range(count)):
        pa0, pb0, pa1, pb1 = ports[k]
        post_a0, post_b0 = pick(k, a0, post_a0), pick(k, b0, post_b0)
        gamma = pb0 / (1.0 - pb1 * a0)
        backward[k] = (gamma, gamma * a0)
        a0, b0 = pa0 + gamma * a0 * pa1, gamma * b0
        from_a0, from_b0 = pick(k, a0, from_a0), pick(k, b0, from_b0)
    lower_scale = 1.0 / (1.0 - pre_b1 * from_a0)
    upper_scale = 1.0 / (1.0 - post_a0 * thru_b1)
    lower = (lower_scale * pre_a1, lower_scale * pre_b1 * from_b0, lower_scale * pre_b1, lower_scale)
    upper = (
        upper_scale * post_a0 * thru_a1,
        upper_scale * post_b0,
        upper_scale * post_a0,
        upper_scale,
    )
    return forward, backward, lower, upper, (a0, b0, a1, b1)


def level_constants(parts, constants, own):
    forward, backward, lower, upper, _ = parts
    count = len(forward)
    nothing = jnp.zeros(TILE, F32)

    def pick(place, new, old):
        return jnp.where(own == place, new, old)

    c1, pre, thru = nothing, nothing, nothing
    for k in range(count):
        k0, k1 = constants[k]
        pre = pick(k, c1, pre)
        beta, beta_b = forward[k]
        c1 = (k1 + beta_b * k0) + beta * c1
        thru = pick(k, c1, thru)
    c0, post, start = nothing, nothing, nothing
    for k in reversed(range(count)):
        k0, k1 = constants[k]
        post = pick(k, c0, post)
        gamma, gamma_a = backward[k]
        c0 = (k0 + gamma_a * k1) + gamma * c0
        start = pick(k, c0, start)
    return c0, c1, lower[2] * start + lower[3] * pre, upper[2] * thru + upper[3] * post


def kernel(
    state_hbm,
    previous_hbm,
    below_hbm,
    above_hbm,
    kappa_hbm,
    new_ref,
    nonlinear_ref,
    state_raw,
    previous_raw,
    sides_raw,
    kappa_ref,
    mix,
    wide,
    tri_x,
    sent_x,
    got_x,
    forcing,
    ports_t,
    ports_h,
    exp_high,
    exp_low,
    angle_cos,
    angle_sin,
    cos_high,
    cos_low,
    leg_high,
    leg_low,
    flip_high,
    flip_low,
    sent_n,
    got_n,
    spread_n,
    shell_q,
    partial,
    green,
    solved,
    port_y,
    const_z,
    const_y,
    relay_sem,
    load_sem,
    x_send,
    x_recv,
    n_send,
    n_recv,
    u_send,
    u_recv,
    py_send,
    py_recv,
    cz_send,
    cz_recv,
    cy_send,
    cy_recv,
):
    row, mode = lax.axis_index("row"), lax.axis_index("lm")
    y, z, core = row // 16, lax.rem(row // 2, 8), lax.rem(row, 2)
    other = row + 1 - 2 * core
    turn = [lax.rem(mode + d, 4) for d in range(4)]
    x_peers = [(row, turn[d]) for d in range(1, 4)]
    core_peers = [(other, turn[d]) for d in range(4)]

    loads = [
        pltpu.make_async_copy(state_hbm, state_raw, load_sem.at[0]),
        pltpu.make_async_copy(previous_hbm, previous_raw, load_sem.at[1]),
        pltpu.make_async_copy(below_hbm, sides_raw.at[0], load_sem.at[2]),
        pltpu.make_async_copy(above_hbm, sides_raw.at[1], load_sem.at[3]),
        pltpu.make_async_copy(kappa_hbm, kappa_ref, load_sem.at[4]),
    ]
    for load in loads:
        load.start()

    def along_z(d):
        return (y * 16 + lax.rem(z + d, 8) * 2 + core, mode)

    def along_y(d):
        return (lax.rem(y + d, 8) * 16 + z * 2 + core, mode)

    z_peers = [along_z(d) for d in (4, 3, 5, 2, 6, 1, 7)]
    y_peers = [along_y(d) for d in (4, 3, 5, 2, 6, 1, 7)]

    barrier = pltpu.get_barrier_semaphore()
    near = x_peers + core_peers + [line(d) for line in (along_z, along_y) for d in (1, 7)]
    for peer in near:
        pl.semaphore_signal(barrier, inc=1, device_id=peer, device_id_type=MESH)

    def relay(step):
        for k, line in enumerate((along_z, along_y)):
            for side, d in enumerate((step, 8 - step)):
                pl.semaphore_signal(
                    relay_sem.at[step - 1, k, side],
                    inc=1,
                    device_id=line(d),
                    device_id_type=MESH,
                )

    def relayed(step):
        for k in range(2):
            for side in range(2):
                pl.semaphore_wait(relay_sem.at[step - 1, k, side], 1)

    def send(source, target, send_sem, recv_sem, peer):
        copy = pltpu.make_async_remote_copy(
            src_ref=source,
            dst_ref=target,
            send_sem=send_sem,
            recv_sem=recv_sem,
            device_id=peer,
            device_id_type=MESH,
        )
        copy.start()
        return copy

    def receive(copies):
        for copy in copies:
            copy.wait_recv()

    source_id, target_id = iota((256, 256), 0), iota((256, 256), 1)
    part = (source_id == 2 * (target_id & 127) + (target_id >> 7)).astype(F32).astype(BF16)
    unite = (target_id == 2 * (source_id & 127) + (source_id >> 7)).astype(F32).astype(BF16)
    sub, lane = iota(TILE, 0), iota(TILE, 1)
    parity, field = sub >> 2, sub & 3
    degree = (mode * 256 + 2 * lane + parity).astype(F32)
    scale = jnp.sqrt(degree + 0.5)

    def to_tiles(values, target):
        for f in range(FIELDS):
            for p in range(2):
                target[pl.ds(p * 4 + f, SHELLS_DEV, stride=8), :] = values[
                    f * 16 : (f + 1) * 16, p * 128 : (p + 1) * 128
                ]

    def from_tiles(source):
        return jnp.concatenate(
            [
                jnp.concatenate(
                    [source[pl.ds(p * 4 + f, SHELLS_DEV, stride=8), :] for p in range(2)], axis=1
                )
                for f in range(FIELDS)
            ],
            axis=0,
        )

    def phase(order, shape):
        return order * (2 * iota(shape, 1) + 1)

    wide_shape = (8, HALF)
    for p, groups in ((0, 7), (1, 4)):
        for group in range(groups):
            turns = phase(32 * (group * 8 + iota(wide_shape, 0)) + p, wide_shape)
            angle_cos[p, group * 8 : group * 8 + 8, :] = 2.0 * cosine(turns)
            angle_sin[p, group * 8 : group * 8 + 8, :] = 2.0 * cosine(turns - NLAT)
    tri_x[...] = jnp.zeros_like(tri_x)
    spread_n[...] = jnp.zeros_like(spread_n)
    wide[...] = jnp.zeros_like(wide)
    loads[0].wait()
    to_tiles(permute_lanes(state_raw[...].reshape(48, 256), part), tri_x)
    wide[...] = (tri_x[...].reshape(SHELLS_DEV, 8, 128) * scale).reshape(128, 128)
    for k in range(4):
        for f in range(FIELDS):
            sent_x[k, f] = wide[pl.ds(k * 32 + f, 8, stride=4), :]
    pl.semaphore_wait(barrier, len(near))
    copies_x = [
        send(
            sent_x.at[peer[1]],
            got_x.at[mode],
            x_send.at[d],
            x_recv.at[d],
            peer,
        )
        for d, peer in enumerate(x_peers)
    ]
    relay(1)
    got_x[mode] = sent_x[mode]

    toeplitz = central_ratio(512 + iota((8, 640), 0) - iota((8, 640), 1))
    hankel = [central_ratio(iota((8, 1024), 0) + iota((8, 1024), 1) + p) for p in range(2)]
    for step in range(16):
        rows = slice(step * 8, step * 8 + 8)
        moved = toeplitz if step == 0 else pltpu.roll(toeplitz, step * 8, 1)
        for b in range(4):
            ports_t[b, rows, :] = moved[:, (4 - b) * 128 : (5 - b) * 128]
        for p in range(2):
            moved = hankel[p] if step == 0 else pltpu.roll(hankel[p], 1024 - step * 8, 1)
            for b in range(7):
                ports_h[p, b, rows, :] = moved[:, b * 128 : (b + 1) * 128]
    for p in range(2):
        for a in range(4):
            for b in range(4):
                here = (p, slice(a * 128, a * 128 + 128), slice(b * 128, b * 128 + 128))
                if b <= a:
                    high, low = split2(ports_t[a - b] * ports_h[p, a + b])
                else:
                    high = low = jnp.zeros((128, 128), BF16)
                exp_high[here] = high
                exp_low[here] = low

    base_shape = (16, HALF)
    turns = phase(2 * iota(base_shape, 0), base_shape)
    base_cos, base_sin = cosine(turns), cosine(turns - NLAT)
    base_row = iota((16, 128), 0)

    def series_term(q):
        order = (16 * q + base_row).astype(F32)
        term = -1.0 / (4.0 * order * order - 1.0)
        term = jnp.where(order > HALF, 0.0, term)
        return jnp.concatenate([term] * (HALF // 128), axis=1)

    def table_rows(p, q):
        return (
            angle_cos[p, pl.ds(q, 1), :] * base_cos - angle_sin[p, pl.ds(q, 1), :] * base_sin
        )

    def fill(q, weight):
        for p in range(2):
            values = table_rows(p, q)
            if p == 0:
                values = jnp.where((iota(base_shape, 0) + 16 * q) == 0, 1.0, values)
                weight = weight + series_term(q) * values
            high, low = split2(values)
            where = pl.ds(pl.multiple_of(q * 16, 16), 16)
            cos_high[p, where, :] = high
            cos_low[p, where, :] = low
        return weight

    weight = lax.fori_loop(0, 32, fill, jnp.zeros(base_shape, F32))
    weight = lax.fori_loop(
        32, 49, lambda q, weight: weight + series_term(q) * table_rows(0, q), weight
    )
    weight = jnp.sum(weight, axis=0, keepdims=True) * (2.0 / NLAT / 16.0)

    for p in range(2):
        for first in (0, 256):
            rows, depth = slice(first, first + 256), first + 256
            top, rest = exp_high[p, rows, :depth], exp_low[p, rows, :depth]
            both = dot(jnp.concatenate([top, rest], axis=0), cos_high[p, :depth, :])
            values = both[:256] + both[256:] + dot(top, cos_low[p, :depth, :])
            for part_of, table, flipped in zip(
                split2(values), (leg_high, leg_low), (flip_high, flip_low)
            ):
                table[p, rows, :] = part_of
                flipped[p, :, rows] = part_of.T

    receive(copies_x)
    even_rows = (iota((32, 1), 0) & 1) == 0
    sign = jnp.where(even_rows, 1.0, -1.0)

    def parities(left, right):
        return jnp.where(even_rows, left, right)

    def swap(values):
        rows = values.shape[0]
        return parities(pltpu.roll(values, rows - 1, 0), pltpu.roll(values, 1, 0))

    spectrum = jnp.concatenate([jnp.concatenate([got_x[k].reshape(24, 128), jnp.zeros(TILE, F32)], axis=0)
            for k in range(4)], axis=1)
    sides = parities(*[dot3(spectrum, leg_high[p], leg_low[p]) for p in range(2)])
    grid = swap(sides) + sign * sides
    velocity, magnetic, thermal = [grid[f * 8 : f * 8 + 8] * weight for f in range(FIELDS)]
    product = jnp.concatenate(
        [
            grid[8:16] * magnetic - grid[:8] * velocity,
            grid[:8] * magnetic,
            -(grid[:8] * thermal),
            jnp.zeros_like(thermal),
        ],
        axis=0,
    )
    folded = swap(product) + sign * product
    terms = parities(*[dot3(folded, flip_high[p], flip_low[p]) for p in range(2)])
    for k in range(4):
        sent_n[k] = terms[:24, k * 128 : (k + 1) * 128].reshape(FIELDS, 8, 128)
    mine = core * 4 + mode
    copies_n = [
        send(sent_n.at[peer[1]], got_n.at[mine], n_send.at[d], n_recv.at[d], peer)
        for d, peer in enumerate(x_peers + core_peers)
    ]
    got_n[mine] = sent_n[mode]
    relayed(1)
    relay(2)

    loads[1].wait()
    to_tiles(permute_lanes(previous_raw[...].reshape(48, 256), part), wide)
    push = 4.0 * SHELLS_DEV * SHELLS_DEV
    forcing[pl.ds(core * SHELLS_DEV, SHELLS_DEV)] = (
        2.0 * tri_x[...] - (0.5 * push) * wide[...]
    ).reshape(SHELLS_DEV, 8, 128)
    copy_u = send(
        forcing.at[pl.ds(core * SHELLS_DEV, SHELLS_DEV)],
        forcing.at[pl.ds(core * SHELLS_DEV, SHELLS_DEV)],
        u_send.at[0],
        u_recv.at[0],
        core_peers[0],
    )

    loads[4].wait()
    kappa = jnp.full(TILE, 1.0, F32)
    for f in range(FIELDS):
        kappa = jnp.where(field == f, kappa_ref[f], kappa)
    alpha = 1.0 / (kappa * (16.0 * SHELLS_DEV * SHELLS_DEV))
    steep = 16.0 * (degree * (degree + 1.0))
    one = jnp.ones(TILE, F32)
    for block in range(SHELLS // 256):
        rho = (iota((256, 128), 0) + block * 256).astype(F32) + (SHELLS + 0.5)
        shell_q[block * 256 : (block + 1) * 256, :] = 1.0 / (rho * rho)

    def beta(shell):
        return alpha + steep * shell_q[pl.ds(shell, 1), :]

    first_shell = (row // 2) * CHIP
    grow, change = one, one
    back, back_change = one, one
    for s in range(CHIP):
        green[1, s] = grow
        change = beta(first_shell + s) * grow + change
        grow = grow + change
        t = CHIP - 1 - s
        green[0, t] = back
        back_change = beta(first_shell + t) * back + back_change
        back = back + back_change
    inverse = 1.0 / grow
    for s in range(CHIP):
        green[0, s] = green[0, s] * inverse
        green[1, s] = green[1, s] * inverse

    def line_ports(line):
        starts = [line * 256 + k * CHIP for k in range(8)]
        carry = []
        for start in starts:
            change = beta(start) + one
            carry += [one + change, change, one, one]

        def step(s, carry):
            after = []
            for k, start in enumerate(starts):
                grow, change, inner, inner_change = carry[4 * k : 4 * k + 4]
                here = beta(start + s)
                change = here * grow + change
                inner_change = here * inner + inner_change
                after += [grow + change, change, inner + inner_change, inner_change]
            return tuple(after)

        carry = lax.fori_loop(1, CHIP, step, tuple(carry))
        ports = []
        for k in range(8):
            grow, change, inner, _ = carry[4 * k : 4 * k + 4]
            tau = 1.0 / grow
            ports.append((inner * tau, tau, tau, (grow - change) * tau))
        return ports

    parts_z = level_parts(line_ports(y), z)
    port_y[y, 0], port_y[y, 1], port_y[y, 2] = parts_z[4][0], parts_z[4][1], parts_z[4][3]

    loads[2].wait()
    loads[3].wait()
    mix[...] = jnp.zeros_like(mix)
    for k in range(2):
        mix[k * 8 : k * 8 + FIELDS, :] = sides_raw[k, :, 0] + sides_raw[k, :, 1]
    parted = permute_lanes(mix[...], part)
    bottom, top = [
        jnp.concatenate([parted[k * 8 : k * 8 + 4, :128], parted[k * 8 : k * 8 + 4, 128:]], axis=0)
        for k in range(2)
    ]
    bottom, top = bottom * (SHELLS - 0.5), top * (2 * SHELLS + 0.5)

    relayed(2)
    copies_py = [
        send(port_y.at[y], port_y.at[y], py_send.at[d], py_recv.at[d], peer)
        for d, peer in enumerate(y_peers)
    ]

    receive([copy_u])
    receive(copies_n)
    for q in range(8):
        for f in range(FIELDS):
            spread_n[pl.ds(q * 32 + f, 8, stride=4), :] = got_n[q, f]
    factor = (1.5 * push) * scale
    sums = [[None] * 4, [None] * 4]
    for s in range(CHIP):
        rho = (first_shell + s).astype(F32) + (SHELLS + 0.5)
        value = (alpha * rho) * (forcing[s] + factor * spread_n[s * 8 : s * 8 + 8, :])
        solved[s] = value
        for k in range(2):
            term = green[k, s] * value
            old = sums[k][s % 4]
            sums[k][s % 4] = term if old is None else old + term
    for k in range(2):
        const_z[z, k] = (sums[k][0] + sums[k][1]) + (sums[k][2] + sums[k][3])
    copies_cz = [
        send(const_z.at[z], const_z.at[z], cz_send.at[d], cz_recv.at[d], peer)
        for d, peer in enumerate(z_peers)
    ]

    run = jnp.zeros(TILE, F32)
    for s in range(CHIP):
        run = run + (green[1, s] * grow) * solved[s]
        partial[s] = green[0, s] * run
    run = jnp.zeros(TILE, F32)
    for s in reversed(range(CHIP)):
        solved_here = solved[s]
        solved[s] = partial[s] + green[1, s] * run
        run = run + (green[0, s] * grow) * solved_here

    wide[...] = (
        spread_n[pl.ds(core * 128, 128), :].reshape(SHELLS_DEV, 8, 128) * scale
    ).reshape(128, 128)
    nonlinear_ref[...] = permute_lanes(from_tiles(wide), unite).reshape(FIELDS, SHELLS_DEV, 256)

    receive(copies_cz)
    total0, total1, lower_z, upper_z = level_constants(
        parts_z, [(const_z[k, 0], const_z[k, 1]) for k in range(8)], z
    )
    const_y[y, 0], const_y[y, 1] = total0, total1
    copies_cy = [
        send(const_y.at[y], const_y.at[y], cy_send.at[d], cy_recv.at[d], peer)
        for d, peer in enumerate(y_peers)
    ]

    own_shells = pl.ds(core * SHELLS_DEV, SHELLS_DEV)
    number = (row * SHELLS_DEV + iota((SHELLS_DEV, 8, 128), 0)).astype(F32) + (SHELLS + 0.5)
    over = 1.0 / number
    rest = solved[own_shells] * over - tri_x[...].reshape(SHELLS_DEV, 8, 128)
    from_low, from_up = green[0, own_shells] * over, green[1, own_shells] * over

    receive(copies_py)
    parts_y = level_parts(
        [(port_y[k, 0], port_y[k, 1], port_y[k, 1], port_y[k, 2]) for k in range(8)], y
    )
    receive(copies_cy)
    _, _, lower_y, upper_y = level_constants(
        parts_y, [(const_y[k, 0], const_y[k, 1]) for k in range(8)], y
    )
    line_low = parts_y[2][0] * bottom + parts_y[2][1] * top + lower_y
    line_up = parts_y[3][0] * bottom + parts_y[3][1] * top + upper_y
    chip_low = parts_z[2][0] * line_low + parts_z[2][1] * line_up + lower_z
    chip_up = parts_z[3][0] * line_low + parts_z[3][1] * line_up + upper_z
    wide[...] = (rest + from_low * chip_low + from_up * chip_up).reshape(128, 128)
    new_ref[...] = permute_lanes(from_tiles(wide), unite).reshape(FIELDS, SHELLS_DEV, 256)

    for copy in copies_x + copies_n + [copy_u] + copies_py + copies_cz + copies_cy:
        copy.wait_send()


def write_out(new_ref, nonlinear_ref, new_hbm, nonlinear_hbm, sem):
    copies = [
        pltpu.make_async_copy(new_ref, new_hbm, sem.at[0]),
        pltpu.make_async_copy(nonlinear_ref, nonlinear_hbm, sem.at[1]),
    ]
    for copy in copies:
        copy.start()
    for copy in copies:
        copy.wait()


def local(state, previous_terms, below, above, kappa):
    block = jax.ShapeDtypeStruct(state.shape, F32)
    vmem, dma = pltpu.VMEM, pltpu.SemaphoreType.DMA
    anywhere = pl.BlockSpec(memory_space=pl.ANY)
    inside = pl.BlockSpec(memory_space=pltpu.VMEM)
    scratch = [
        vmem((FIELDS, SHELLS_DEV, 256), F32),
        vmem((FIELDS, SHELLS_DEV, 256), F32),
        vmem((2, FIELDS, 2, 256), F32),
        pltpu.SMEM((FIELDS,), F32),
        vmem((16, 256), F32),
        vmem((128, 128), F32),
        vmem((128, 128), F32),
        vmem((4, FIELDS, 8, 128), F32),
        vmem((4, FIELDS, 8, 128), F32),
        vmem((CHIP, 8, 128), F32),
        vmem((4, 128, 128), F32),
        vmem((2, 7, 128, 128), F32),
        vmem((2, PAIRS, PAIRS), BF16),
        vmem((2, PAIRS, PAIRS), BF16),
        vmem((2, 56, HALF), F32),
        vmem((2, 56, HALF), F32),
        vmem((2, PAIRS, HALF), BF16),
        vmem((2, PAIRS, HALF), BF16),
        vmem((2, PAIRS, HALF), BF16),
        vmem((2, PAIRS, HALF), BF16),
        vmem((2, HALF, PAIRS), BF16),
        vmem((2, HALF, PAIRS), BF16),
        vmem((4, FIELDS, 8, 128), F32),
        vmem((8, FIELDS, 8, 128), F32),
        vmem((CHIP * 8, 128), F32),
        vmem((SHELLS, 128), F32),
        vmem((CHIP, 8, 128), F32),
        vmem((2, CHIP, 8, 128), F32),
        vmem((CHIP, 8, 128), F32),
        vmem((8, 3, 8, 128), F32),
        vmem((8, 2, 8, 128), F32),
        vmem((8, 2, 8, 128), F32),
        pltpu.SemaphoreType.REGULAR((2, 2, 2)),
        dma((5,)),
        dma((3,)),
        dma((3,)),
        dma((7,)),
        dma((7,)),
        dma((1,)),
        dma((1,)),
    ] + [dma((7,))] * 6
    held = pltpu.VMEM(state.shape, F32)
    operands = [
        pltpu.with_memory_space_constraint(operand, pltpu.HBM)
        for operand in (
            state,
            previous_terms,
            jnp.transpose(below, (1, 0, 2)),
            jnp.transpose(above, (1, 0, 2)),
            kappa,
        )
    ]
    results = pl.pallas_call(
        kernel,
        out_shape=(held, held),
        in_specs=[anywhere] * 5,
        out_specs=(inside, inside),
        scratch_shapes=scratch,
        compiler_params=pltpu.CompilerParams(
            collective_id=0, has_side_effects=True, vmem_limit_bytes=32 * 1024 * 1024
        ),
    )(*operands)
    return pl.pallas_call(
        write_out,
        out_shape=(block, block),
        in_specs=[inside] * 2,
        out_specs=(anywhere, anywhere),
        scratch_shapes=[dma((2,))],
    )(*[pltpu.with_memory_space_constraint(result, pltpu.VMEM) for result in results])


def solution(mesh):
    in_specs = (
        P(None, "row", "lm"),
        P(None, "row", "lm"),
        P(None, None, "lm"),
        P(None, None, "lm"),
        P(),
    )
    out_specs = (P(None, "row", "lm"), P(None, "row", "lm"))
    return jax.shard_map(local, mesh=mesh, in_specs=in_specs, out_specs=out_specs, check_vma=False)
```

```python
import functools
import math

import jax
import jax.numpy as jnp
from jax import lax
from jax.experimental import pallas as pl
from jax.experimental.pallas import tpu as pltpu
from jax.sharding import PartitionSpec as P

MESH = pl.DeviceIdType.MESH
F32, BF16 = jnp.float32, jnp.bfloat16
NLAT = 1536
HALF = NLAT // 2
DEGREES = 1024
PAIRS = DEGREES // 2
SHELLS = 2048
SHELLS_DEV = 16
CHIP = 2 * SHELLS_DEV
FIELDS = 3
TILE = (8, 128)
CENTRAL_TERMS = [math.comb(2 * k, k) / 4.0**k for k in range(16)]


def central_ratio(counts):
    number = counts.astype(F32)
    bigger = jnp.maximum(number, 1.0)
    inverse = 1.0 / bigger
    series = 1.0 + inverse * (
        -0.125 + inverse * (0.0078125 + inverse * (0.0048828125 - inverse * 0.000640869140625))
    )
    result = series / jnp.sqrt(math.pi * bigger)
    for k in range(16):
        result = jnp.where(counts == k, CENTRAL_TERMS[k], result)
    return jnp.where(counts < 0, 0.0, result)


def cosine(phase):
    turn = 4.0 * NLAT
    number = phase.astype(F32)
    number = number - turn * jnp.floor(number * (1.0 / turn) + 0.5)
    angle = (NLAT - jnp.abs(number)) * (math.pi / (2 * NLAT))
    square = angle * angle
    total = jnp.full_like(square, 1.0 / math.factorial(13))
    for order in (11, 9, 7, 5, 3, 1):
        sign = -1.0 if order % 4 == 3 else 1.0
        total = sign / math.factorial(order) + square * total
    return angle * total


def split2(value):
    high = value.astype(BF16)
    low = (value - high.astype(F32)).astype(BF16)
    return high, low


def dot(left, right, transposed=False):
    dims = (((1,), (1 if transposed else 0,)), ((), ()))
    return lax.dot_general(left, right, dims, preferred_element_type=F32)


def dot3(left, high, low, transposed=False):
    rows = left.shape[0]
    top, rest = split2(left)
    both = dot(jnp.concatenate([top, rest], axis=0), high, transposed)
    return both[:rows] + both[rows:] + dot(top, low, transposed)


def permute_lanes(value, matrix):
    rows = value.shape[0]
    first = value.astype(BF16)
    left = value - first.astype(F32)
    second = left.astype(BF16)
    third = (left - second.astype(F32)).astype(BF16)
    out = dot(jnp.concatenate([first, second, third], axis=0), matrix)
    return out[:rows] + out[rows : 2 * rows] + out[2 * rows :]


def iota(shape, axis):
    return lax.broadcasted_iota(jnp.int32, shape, axis)


def level_parts(ports, own):
    count = len(ports)
    one, nothing = jnp.ones(TILE, F32), jnp.zeros(TILE, F32)

    def pick(place, new, old):
        return jnp.where(own == place, new, old)

    forward, backward = [None] * count, [None] * count
    a1, b1 = one, nothing
    pre_a1, pre_b1, thru_a1, thru_b1 = one, nothing, one, nothing
    for k in range(count):
        pa0, pb0, pa1, pb1 = ports[k]
        pre_a1, pre_b1 = pick(k, a1, pre_a1), pick(k, b1, pre_b1)
        beta = pa1 / (1.0 - b1 * pa0)
        forward[k] = (beta, beta * b1)
        a1, b1 = beta * a1, pb1 + beta * b1 * pb0
        thru_a1, thru_b1 = pick(k, a1, thru_a1), pick(k, b1, thru_b1)
    a0, b0 = nothing, one
    post_a0, post_b0, from_a0, from_b0 = nothing, one, nothing, one
    for k in reversed(range(count)):
        pa0, pb0, pa1, pb1 = ports[k]
        post_a0, post_b0 = pick(k, a0, post_a0), pick(k, b0, post_b0)
        gamma = pb0 / (1.0 - pb1 * a0)
        backward[k] = (gamma, gamma * a0)
        a0, b0 = pa0 + gamma * a0 * pa1, gamma * b0
        from_a0, from_b0 = pick(k, a0, from_a0), pick(k, b0, from_b0)
    lower_scale = 1.0 / (1.0 - pre_b1 * from_a0)
    upper_scale = 1.0 / (1.0 - post_a0 * thru_b1)
    lower = (lower_scale * pre_a1, lower_scale * pre_b1 * from_b0, lower_scale * pre_b1, lower_scale)
    upper = (
        upper_scale * post_a0 * thru_a1,
        upper_scale * post_b0,
        upper_scale * post_a0,
        upper_scale,
    )
    return forward, backward, lower, upper, (a0, b0, a1, b1)


def level_constants(parts, constants, own):
    forward, backward, lower, upper, _ = parts
    count = len(forward)
    nothing = jnp.zeros(TILE, F32)

    def pick(place, new, old):
        return jnp.where(own == place, new, old)

    c1, pre, thru = nothing, nothing, nothing
    for k in range(count):
        k0, k1 = constants[k]
        pre = pick(k, c1, pre)
        beta, beta_b = forward[k]
        c1 = (k1 + beta_b * k0) + beta * c1
        thru = pick(k, c1, thru)
    c0, post, start = nothing, nothing, nothing
    for k in reversed(range(count)):
        k0, k1 = constants[k]
        post = pick(k, c0, post)
        gamma, gamma_a = backward[k]
        c0 = (k0 + gamma_a * k1) + gamma * c0
        start = pick(k, c0, start)
    return c0, c1, lower[2] * start + lower[3] * pre, upper[2] * thru + upper[3] * post


def kernel(
    state_hbm,
    previous_hbm,
    below_hbm,
    above_hbm,
    kappa_hbm,
    new_ref,
    nonlinear_ref,
    state_raw,
    previous_raw,
    sides_raw,
    kappa_ref,
    mix,
    wide,
    tri_x,
    sent_x,
    got_x,
    forcing,
    ports_t,
    ports_h,
    exp_high,
    exp_low,
    angle_cos,
    angle_sin,
    cos_high,
    cos_low,
    leg_high,
    leg_low,
    flip_high,
    flip_low,
    sent_n,
    got_n,
    spread_n,
    shell_q,
    partial,
    green,
    solved,
    port_y,
    const_z,
    const_y,
    relay_sem,
    load_sem,
    x_send,
    x_recv,
    n_send,
    n_recv,
    u_send,
    u_recv,
    py_send,
    py_recv,
    cz_send,
    cz_recv,
    cy_send,
    cy_recv,
):
    row, mode = lax.axis_index("row"), lax.axis_index("lm")
    y, z, core = row // 16, lax.rem(row // 2, 8), lax.rem(row, 2)
    other = row + 1 - 2 * core
    turn = [lax.rem(mode + d, 4) for d in range(4)]
    x_peers = [(row, turn[d]) for d in range(1, 4)]
    core_peers = [(other, turn[d]) for d in range(4)]

    loads = [
        pltpu.make_async_copy(state_hbm, state_raw, load_sem.at[0]),
        pltpu.make_async_copy(previous_hbm, previous_raw, load_sem.at[1]),
        pltpu.make_async_copy(below_hbm, sides_raw.at[0], load_sem.at[2]),
        pltpu.make_async_copy(above_hbm, sides_raw.at[1], load_sem.at[3]),
        pltpu.make_async_copy(kappa_hbm, kappa_ref, load_sem.at[4]),
    ]
    for load in loads:
        load.start()

    def along_z(d):
        return (y * 16 + lax.rem(z + d, 8) * 2 + core, mode)

    def along_y(d):
        return (lax.rem(y + d, 8) * 16 + z * 2 + core, mode)

    z_peers = [along_z(d) for d in (4, 3, 5, 2, 6, 1, 7)]
    y_peers = [along_y(d) for d in (4, 3, 5, 2, 6, 1, 7)]

    barrier = pltpu.get_barrier_semaphore()
    near = x_peers + core_peers + [line(d) for line in (along_z, along_y) for d in (1, 7)]
    for peer in near:
        pl.semaphore_signal(barrier, inc=1, device_id=peer, device_id_type=MESH)

    def relay(step):
        for k, line in enumerate((along_z, along_y)):
            for side, d in enumerate((step, 8 - step)):
                pl.semaphore_signal(
                    relay_sem.at[step - 1, k, side],
                    inc=1,
                    device_id=line(d),
                    device_id_type=MESH,
                )

    def relayed(step):
        for k in range(2):
            for side in range(2):
                pl.semaphore_wait(relay_sem.at[step - 1, k, side], 1)

    def send(source, target, send_sem, recv_sem, peer):
        copy = pltpu.make_async_remote_copy(
            src_ref=source,
            dst_ref=target,
            send_sem=send_sem,
            recv_sem=recv_sem,
            device_id=peer,
            device_id_type=MESH,
        )
        copy.start()
        return copy

    def receive(copies):
        for copy in copies:
            copy.wait_recv()

    source_id, target_id = iota((256, 256), 0), iota((256, 256), 1)
    part = (source_id == 2 * (target_id & 127) + (target_id >> 7)).astype(F32).astype(BF16)
    unite = (target_id == 2 * (source_id & 127) + (source_id >> 7)).astype(F32).astype(BF16)
    sub, lane = iota(TILE, 0), iota(TILE, 1)
    parity, field = sub >> 2, sub & 3
    degree = (mode * 256 + 2 * lane + parity).astype(F32)
    scale = jnp.sqrt(degree + 0.5)

    def to_tiles(values, target):
        for f in range(FIELDS):
            for p in range(2):
                target[pl.ds(p * 4 + f, SHELLS_DEV, stride=8), :] = values[
                    f * 16 : (f + 1) * 16, p * 128 : (p + 1) * 128
                ]

    def from_tiles(source):
        return jnp.concatenate(
            [
                jnp.concatenate(
                    [source[pl.ds(p * 4 + f, SHELLS_DEV, stride=8), :] for p in range(2)], axis=1
                )
                for f in range(FIELDS)
            ],
            axis=0,
        )

    def phase(order, shape):
        return order * (2 * iota(shape, 1) + 1)

    wide_shape = (8, HALF)
    for p, groups in ((0, 7), (1, 4)):
        for group in range(groups):
            turns = phase(32 * (group * 8 + iota(wide_shape, 0)) + p, wide_shape)
            angle_cos[p, group * 8 : group * 8 + 8, :] = 2.0 * cosine(turns)
            angle_sin[p, group * 8 : group * 8 + 8, :] = 2.0 * cosine(turns - NLAT)
    tri_x[...] = jnp.zeros_like(tri_x)
    spread_n[...] = jnp.zeros_like(spread_n)
    wide[...] = jnp.zeros_like(wide)
    loads[0].wait()
    to_tiles(permute_lanes(state_raw[...].reshape(48, 256), part), tri_x)
    wide[...] = (tri_x[...].reshape(SHELLS_DEV, 8, 128) * scale).reshape(128, 128)
    for k in range(4):
        for f in range(FIELDS):
            sent_x[k, f] = wide[pl.ds(k * 32 + f, 8, stride=4), :]
    pl.semaphore_wait(barrier, len(near))
    copies_x = [
        send(
            sent_x.at[peer[1]],
            got_x.at[mode],
            x_send.at[d],
            x_recv.at[d],
            peer,
        )
        for d, peer in enumerate(x_peers)
    ]
    relay(1)
    got_x[mode] = sent_x[mode]

    toeplitz = central_ratio(512 + iota((8, 640), 0) - iota((8, 640), 1))
    hankel = [central_ratio(iota((8, 1024), 0) + iota((8, 1024), 1) + p) for p in range(2)]
    for step in range(16):
        rows = slice(step * 8, step * 8 + 8)
        moved = toeplitz if step == 0 else pltpu.roll(toeplitz, step * 8, 1)
        for b in range(4):
            ports_t[b, rows, :] = moved[:, (4 - b) * 128 : (5 - b) * 128]
        for p in range(2):
            moved = hankel[p] if step == 0 else pltpu.roll(hankel[p], 1024 - step * 8, 1)
            for b in range(7):
                ports_h[p, b, rows, :] = moved[:, b * 128 : (b + 1) * 128]
    for p in range(2):
        for a in range(4):
            for b in range(4):
                here = (p, slice(a * 128, a * 128 + 128), slice(b * 128, b * 128 + 128))
                if b <= a:
                    high, low = split2(ports_t[a - b] * ports_h[p, a + b])
                else:
                    high = low = jnp.zeros((128, 128), BF16)
                exp_high[here] = high
                exp_low[here] = low

    base_shape = (16, HALF)
    turns = phase(2 * iota(base_shape, 0), base_shape)
    base_cos, base_sin = cosine(turns), cosine(turns - NLAT)
    def fill(q, unused):
        for p in range(2):
            row_cos, row_sin = angle_cos[p, pl.ds(q, 1), :], angle_sin[p, pl.ds(q, 1), :]
            values = row_cos * base_cos - row_sin * base_sin
            if p == 0:
                values = jnp.where((iota(base_shape, 0) + 16 * q) == 0, 1.0, values)
            high, low = split2(values)
            where = pl.ds(pl.multiple_of(q * 16, 16), 16)
            cos_high[p, where, :] = high
            cos_low[p, where, :] = low
        return unused

    lax.fori_loop(0, 32, fill, 0)
    order = (iota((16, 56), 0) + 16 * iota((16, 56), 1)).astype(F32)
    series = jnp.where(order > HALF, 0.0, -1.0 / (4.0 * order * order - 1.0))
    series = jnp.where(order == 0.0, 0.5, series)
    over_cos, over_sin = [
        jnp.dot(series, rows[0], precision=lax.Precision.HIGHEST, preferred_element_type=F32)
        for rows in (angle_cos, angle_sin)
    ]
    weight = jnp.sum(over_cos * base_cos - over_sin * base_sin, axis=0, keepdims=True)
    weight = weight * (2.0 / NLAT / 16.0)

    for p in range(2):
        for first in (0, 256):
            rows, depth = slice(first, first + 256), first + 256
            top, rest = exp_high[p, rows, :depth], exp_low[p, rows, :depth]
            both = dot(jnp.concatenate([top, rest], axis=0), cos_high[p, :depth, :])
            values = both[:256] + both[256:] + dot(top, cos_low[p, :depth, :])
            for part_of, table, flipped in zip(
                split2(values), (leg_high, leg_low), (flip_high, flip_low)
            ):
                table[p, rows, :] = part_of
                flipped[p, :, rows] = part_of.T

    receive(copies_x)
    even_rows = (iota((32, 1), 0) & 1) == 0
    sign = jnp.where(even_rows, 1.0, -1.0)

    def parities(left, right):
        return jnp.where(even_rows, left, right)

    def swap(values):
        rows = values.shape[0]
        return parities(pltpu.roll(values, rows - 1, 0), pltpu.roll(values, 1, 0))

    spectrum = jnp.concatenate([jnp.concatenate([got_x[k].reshape(24, 128), jnp.zeros(TILE, F32)], axis=0)
            for k in range(4)], axis=1)
    sides = parities(*[dot3(spectrum, leg_high[p], leg_low[p]) for p in range(2)])
    grid = swap(sides) + sign * sides
    velocity, magnetic, thermal = [grid[f * 8 : f * 8 + 8] * weight for f in range(FIELDS)]
    product = jnp.concatenate(
        [
            grid[8:16] * magnetic - grid[:8] * velocity,
            grid[:8] * magnetic,
            -(grid[:8] * thermal),
            jnp.zeros_like(thermal),
        ],
        axis=0,
    )
    folded = swap(product) + sign * product
    terms = parities(*[dot3(folded, flip_high[p], flip_low[p]) for p in range(2)])
    for k in range(4):
        sent_n[k] = terms[:24, k * 128 : (k + 1) * 128].reshape(FIELDS, 8, 128)
    mine = core * 4 + mode
    copies_n = [
        send(sent_n.at[peer[1]], got_n.at[mine], n_send.at[d], n_recv.at[d], peer)
        for d, peer in enumerate(x_peers + core_peers)
    ]
    got_n[mine] = sent_n[mode]
    relayed(1)
    relay(2)

    loads[1].wait()
    to_tiles(permute_lanes(previous_raw[...].reshape(48, 256), part), wide)
    push = 4.0 * SHELLS_DEV * SHELLS_DEV
    forcing[pl.ds(core * SHELLS_DEV, SHELLS_DEV)] = (
        2.0 * tri_x[...] - (0.5 * push) * wide[...]
    ).reshape(SHELLS_DEV, 8, 128)
    copy_u = send(
        forcing.at[pl.ds(core * SHELLS_DEV, SHELLS_DEV)],
        forcing.at[pl.ds(core * SHELLS_DEV, SHELLS_DEV)],
        u_send.at[0],
        u_recv.at[0],
        core_peers[0],
    )

    loads[4].wait()
    kappa = jnp.full(TILE, 1.0, F32)
    for f in range(FIELDS):
        kappa = jnp.where(field == f, kappa_ref[f], kappa)
    alpha = 1.0 / (kappa * (16.0 * SHELLS_DEV * SHELLS_DEV))
    steep = 16.0 * (degree * (degree + 1.0))
    one = jnp.ones(TILE, F32)
    for block in range(SHELLS // 256):
        rho = (iota((256, 128), 0) + block * 256).astype(F32) + (SHELLS + 0.5)
        shell_q[block * 256 : (block + 1) * 256, :] = 1.0 / (rho * rho)

    def beta(shell):
        return alpha + steep * shell_q[pl.ds(shell, 1), :]

    first_shell = (row // 2) * CHIP
    grow, change = one, one
    back, back_change = one, one
    for s in range(CHIP):
        green[1, s] = grow
        change = beta(first_shell + s) * grow + change
        grow = grow + change
        t = CHIP - 1 - s
        green[0, t] = back
        back_change = beta(first_shell + t) * back + back_change
        back = back + back_change
    inverse = 1.0 / grow
    for s in range(CHIP):
        green[0, s] = green[0, s] * inverse
        green[1, s] = green[1, s] * inverse

    def line_ports(line):
        starts = [line * 256 + k * CHIP for k in range(8)]
        carry = []
        for start in starts:
            change = beta(start) + one
            carry += [one + change, change, one, one]

        def step(s, carry):
            after = []
            for k, start in enumerate(starts):
                grow, change, inner, inner_change = carry[4 * k : 4 * k + 4]
                here = beta(start + s)
                change = here * grow + change
                inner_change = here * inner + inner_change
                after += [grow + change, change, inner + inner_change, inner_change]
            return tuple(after)

        carry = lax.fori_loop(1, CHIP, step, tuple(carry))
        ports = []
        for k in range(8):
            grow, change, inner, _ = carry[4 * k : 4 * k + 4]
            tau = 1.0 / grow
            ports.append((inner * tau, tau, tau, (grow - change) * tau))
        return ports

    parts_z = level_parts(line_ports(y), z)
    port_y[y, 0], port_y[y, 1], port_y[y, 2] = parts_z[4][0], parts_z[4][1], parts_z[4][3]

    loads[2].wait()
    loads[3].wait()
    mix[...] = jnp.zeros_like(mix)
    for k in range(2):
        mix[k * 8 : k * 8 + FIELDS, :] = sides_raw[k, :, 0] + sides_raw[k, :, 1]
    parted = permute_lanes(mix[...], part)
    bottom, top = [
        jnp.concatenate([parted[k * 8 : k * 8 + 4, :128], parted[k * 8 : k * 8 + 4, 128:]], axis=0)
        for k in range(2)
    ]
    bottom, top = bottom * (SHELLS - 0.5), top * (2 * SHELLS + 0.5)

    relayed(2)
    copies_py = [
        send(port_y.at[y], port_y.at[y], py_send.at[d], py_recv.at[d], peer)
        for d, peer in enumerate(y_peers)
    ]

    receive([copy_u])
    receive(copies_n)
    for q in range(8):
        for f in range(FIELDS):
            spread_n[pl.ds(q * 32 + f, 8, stride=4), :] = got_n[q, f]
    factor = (1.5 * push) * scale
    sums = [[None] * 4, [None] * 4]
    for s in range(CHIP):
        rho = (first_shell + s).astype(F32) + (SHELLS + 0.5)
        value = (alpha * rho) * (forcing[s] + factor * spread_n[s * 8 : s * 8 + 8, :])
        solved[s] = value
        for k in range(2):
            term = green[k, s] * value
            old = sums[k][s % 4]
            sums[k][s % 4] = term if old is None else old + term
    for k in range(2):
        const_z[z, k] = (sums[k][0] + sums[k][1]) + (sums[k][2] + sums[k][3])
    copies_cz = [
        send(const_z.at[z], const_z.at[z], cz_send.at[d], cz_recv.at[d], peer)
        for d, peer in enumerate(z_peers)
    ]

    run = jnp.zeros(TILE, F32)
    for s in range(CHIP):
        run = run + (green[1, s] * grow) * solved[s]
        partial[s] = green[0, s] * run
    run = jnp.zeros(TILE, F32)
    for s in reversed(range(CHIP)):
        solved_here = solved[s]
        solved[s] = partial[s] + green[1, s] * run
        run = run + (green[0, s] * grow) * solved_here

    wide[...] = (
        spread_n[pl.ds(core * 128, 128), :].reshape(SHELLS_DEV, 8, 128) * scale
    ).reshape(128, 128)
    nonlinear_ref[...] = permute_lanes(from_tiles(wide), unite).reshape(FIELDS, SHELLS_DEV, 256)

    receive(copies_cz)
    total0, total1, lower_z, upper_z = level_constants(
        parts_z, [(const_z[k, 0], const_z[k, 1]) for k in range(8)], z
    )
    const_y[y, 0], const_y[y, 1] = total0, total1
    copies_cy = [
        send(const_y.at[y], const_y.at[y], cy_send.at[d], cy_recv.at[d], peer)
        for d, peer in enumerate(y_peers)
    ]

    own_shells = pl.ds(core * SHELLS_DEV, SHELLS_DEV)
    number = (row * SHELLS_DEV + iota((SHELLS_DEV, 8, 128), 0)).astype(F32) + (SHELLS + 0.5)
    over = 1.0 / number
    rest = solved[own_shells] * over - tri_x[...].reshape(SHELLS_DEV, 8, 128)
    from_low, from_up = green[0, own_shells] * over, green[1, own_shells] * over

    receive(copies_py)
    parts_y = level_parts(
        [(port_y[k, 0], port_y[k, 1], port_y[k, 1], port_y[k, 2]) for k in range(8)], y
    )
    receive(copies_cy)
    _, _, lower_y, upper_y = level_constants(
        parts_y, [(const_y[k, 0], const_y[k, 1]) for k in range(8)], y
    )
    line_low = parts_y[2][0] * bottom + parts_y[2][1] * top + lower_y
    line_up = parts_y[3][0] * bottom + parts_y[3][1] * top + upper_y
    chip_low = parts_z[2][0] * line_low + parts_z[2][1] * line_up + lower_z
    chip_up = parts_z[3][0] * line_low + parts_z[3][1] * line_up + upper_z
    wide[...] = (rest + from_low * chip_low + from_up * chip_up).reshape(128, 128)
    new_ref[...] = permute_lanes(from_tiles(wide), unite).reshape(FIELDS, SHELLS_DEV, 256)

    for copy in copies_x + copies_n + [copy_u] + copies_py + copies_cz + copies_cy:
        copy.wait_send()


def write_out(new_ref, nonlinear_ref, new_hbm, nonlinear_hbm, sem):
    copies = [
        pltpu.make_async_copy(new_ref, new_hbm, sem.at[0]),
        pltpu.make_async_copy(nonlinear_ref, nonlinear_hbm, sem.at[1]),
    ]
    for copy in copies:
        copy.start()
    for copy in copies:
        copy.wait()


def local(state, previous_terms, below, above, kappa):
    block = jax.ShapeDtypeStruct(state.shape, F32)
    vmem, dma = pltpu.VMEM, pltpu.SemaphoreType.DMA
    anywhere = pl.BlockSpec(memory_space=pl.ANY)
    inside = pl.BlockSpec(memory_space=pltpu.VMEM)
    scratch = [
        vmem((FIELDS, SHELLS_DEV, 256), F32),
        vmem((FIELDS, SHELLS_DEV, 256), F32),
        vmem((2, FIELDS, 2, 256), F32),
        pltpu.SMEM((FIELDS,), F32),
        vmem((16, 256), F32),
        vmem((128, 128), F32),
        vmem((128, 128), F32),
        vmem((4, FIELDS, 8, 128), F32),
        vmem((4, FIELDS, 8, 128), F32),
        vmem((CHIP, 8, 128), F32),
        vmem((4, 128, 128), F32),
        vmem((2, 7, 128, 128), F32),
        vmem((2, PAIRS, PAIRS), BF16),
        vmem((2, PAIRS, PAIRS), BF16),
        vmem((2, 56, HALF), F32),
        vmem((2, 56, HALF), F32),
        vmem((2, PAIRS, HALF), BF16),
        vmem((2, PAIRS, HALF), BF16),
        vmem((2, PAIRS, HALF), BF16),
        vmem((2, PAIRS, HALF), BF16),
        vmem((2, HALF, PAIRS), BF16),
        vmem((2, HALF, PAIRS), BF16),
        vmem((4, FIELDS, 8, 128), F32),
        vmem((8, FIELDS, 8, 128), F32),
        vmem((CHIP * 8, 128), F32),
        vmem((SHELLS, 128), F32),
        vmem((CHIP, 8, 128), F32),
        vmem((2, CHIP, 8, 128), F32),
        vmem((CHIP, 8, 128), F32),
        vmem((8, 3, 8, 128), F32),
        vmem((8, 2, 8, 128), F32),
        vmem((8, 2, 8, 128), F32),
        pltpu.SemaphoreType.REGULAR((2, 2, 2)),
        dma((5,)),
        dma((3,)),
        dma((3,)),
        dma((7,)),
        dma((7,)),
        dma((1,)),
        dma((1,)),
    ] + [dma((7,))] * 6
    held = pltpu.VMEM(state.shape, F32)
    operands = [
        pltpu.with_memory_space_constraint(operand, pltpu.HBM)
        for operand in (
            state,
            previous_terms,
            jnp.transpose(below, (1, 0, 2)),
            jnp.transpose(above, (1, 0, 2)),
            kappa,
        )
    ]
    results = pl.pallas_call(
        kernel,
        out_shape=(held, held),
        in_specs=[anywhere] * 5,
        out_specs=(inside, inside),
        scratch_shapes=scratch,
        compiler_params=pltpu.CompilerParams(
            collective_id=0, has_side_effects=True, vmem_limit_bytes=32 * 1024 * 1024
        ),
    )(*operands)
    return pl.pallas_call(
        write_out,
        out_shape=(block, block),
        in_specs=[inside] * 2,
        out_specs=(anywhere, anywhere),
        scratch_shapes=[dma((2,))],
    )(*[pltpu.with_memory_space_constraint(result, pltpu.VMEM) for result in results])


def solution(mesh):
    in_specs = (
        P(None, "row", "lm"),
        P(None, "row", "lm"),
        P(None, None, "lm"),
        P(None, None, "lm"),
        P(),
    )
    out_specs = (P(None, "row", "lm"), P(None, "row", "lm"))
    return jax.shard_map(local, mesh=mesh, in_specs=in_specs, out_specs=out_specs, check_vma=False)
```

```python
import functools
import math

import jax
import jax.numpy as jnp
from jax import lax
from jax.experimental import pallas as pl
from jax.experimental.pallas import tpu as pltpu
from jax.sharding import PartitionSpec as P

MESH = pl.DeviceIdType.MESH
F32, BF16 = jnp.float32, jnp.bfloat16
NLAT = 1536
HALF = NLAT // 2
DEGREES = 1024
PAIRS = DEGREES // 2
SHELLS = 2048
SHELLS_DEV = 16
CHIP = 2 * SHELLS_DEV
FIELDS = 3
TILE = (8, 128)
CENTRAL_TERMS = [math.comb(2 * k, k) / 4.0**k for k in range(16)]


def central_ratio(counts):
    number = counts.astype(F32)
    bigger = jnp.maximum(number, 1.0)
    inverse = 1.0 / bigger
    series = 1.0 + inverse * (
        -0.125 + inverse * (0.0078125 + inverse * (0.0048828125 - inverse * 0.000640869140625))
    )
    result = series / jnp.sqrt(math.pi * bigger)
    for k in range(16):
        result = jnp.where(counts == k, CENTRAL_TERMS[k], result)
    return jnp.where(counts < 0, 0.0, result)


def cosine(phase):
    turn = 4.0 * NLAT
    number = phase.astype(F32)
    number = number - turn * jnp.floor(number * (1.0 / turn) + 0.5)
    angle = (NLAT - jnp.abs(number)) * (math.pi / (2 * NLAT))
    square = angle * angle
    total = jnp.full_like(square, 1.0 / math.factorial(13))
    for order in (11, 9, 7, 5, 3, 1):
        sign = -1.0 if order % 4 == 3 else 1.0
        total = sign / math.factorial(order) + square * total
    return angle * total


def split2(value):
    high = value.astype(BF16)
    low = (value - high.astype(F32)).astype(BF16)
    return high, low


def dot(left, right, transposed=False):
    dims = (((1,), (1 if transposed else 0,)), ((), ()))
    return lax.dot_general(left, right, dims, preferred_element_type=F32)


def dot3(left, high, low, transposed=False):
    rows = left.shape[0]
    top, rest = split2(left)
    both = dot(jnp.concatenate([top, rest], axis=0), high, transposed)
    return both[:rows] + both[rows:] + dot(top, low, transposed)


def permute_lanes(value, matrix):
    rows = value.shape[0]
    first = value.astype(BF16)
    left = value - first.astype(F32)
    second = left.astype(BF16)
    third = (left - second.astype(F32)).astype(BF16)
    out = dot(jnp.concatenate([first, second, third], axis=0), matrix)
    return out[:rows] + out[rows : 2 * rows] + out[2 * rows :]


def iota(shape, axis):
    return lax.broadcasted_iota(jnp.int32, shape, axis)


def level_parts(ports, own):
    count = len(ports)
    one, nothing = jnp.ones(TILE, F32), jnp.zeros(TILE, F32)

    def pick(place, new, old):
        return jnp.where(own == place, new, old)

    forward, backward = [None] * count, [None] * count
    a1, b1 = one, nothing
    pre_a1, pre_b1, thru_a1, thru_b1 = one, nothing, one, nothing
    for k in range(count):
        pa0, pb0, pa1, pb1 = ports[k]
        pre_a1, pre_b1 = pick(k, a1, pre_a1), pick(k, b1, pre_b1)
        beta = pa1 / (1.0 - b1 * pa0)
        forward[k] = (beta, beta * b1)
        a1, b1 = beta * a1, pb1 + beta * b1 * pb0
        thru_a1, thru_b1 = pick(k, a1, thru_a1), pick(k, b1, thru_b1)
    a0, b0 = nothing, one
    post_a0, post_b0, from_a0, from_b0 = nothing, one, nothing, one
    for k in reversed(range(count)):
        pa0, pb0, pa1, pb1 = ports[k]
        post_a0, post_b0 = pick(k, a0, post_a0), pick(k, b0, post_b0)
        gamma = pb0 / (1.0 - pb1 * a0)
        backward[k] = (gamma, gamma * a0)
        a0, b0 = pa0 + gamma * a0 * pa1, gamma * b0
        from_a0, from_b0 = pick(k, a0, from_a0), pick(k, b0, from_b0)
    lower_scale = 1.0 / (1.0 - pre_b1 * from_a0)
    upper_scale = 1.0 / (1.0 - post_a0 * thru_b1)
    lower = (lower_scale * pre_a1, lower_scale * pre_b1 * from_b0, lower_scale * pre_b1, lower_scale)
    upper = (
        upper_scale * post_a0 * thru_a1,
        upper_scale * post_b0,
        upper_scale * post_a0,
        upper_scale,
    )
    return forward, backward, lower, upper, (a0, b0, a1, b1)


def level_constants(parts, constants, own):
    forward, backward, lower, upper, _ = parts
    count = len(forward)
    nothing = jnp.zeros(TILE, F32)

    def pick(place, new, old):
        return jnp.where(own == place, new, old)

    c1, pre, thru = nothing, nothing, nothing
    for k in range(count):
        k0, k1 = constants[k]
        pre = pick(k, c1, pre)
        beta, beta_b = forward[k]
        c1 = (k1 + beta_b * k0) + beta * c1
        thru = pick(k, c1, thru)
    c0, post, start = nothing, nothing, nothing
    for k in reversed(range(count)):
        k0, k1 = constants[k]
        post = pick(k, c0, post)
        gamma, gamma_a = backward[k]
        c0 = (k0 + gamma_a * k1) + gamma * c0
        start = pick(k, c0, start)
    return c0, c1, lower[2] * start + lower[3] * pre, upper[2] * thru + upper[3] * post


def kernel(
    state_hbm,
    previous_hbm,
    below_hbm,
    above_hbm,
    kappa_hbm,
    new_ref,
    nonlinear_ref,
    state_raw,
    previous_raw,
    sides_raw,
    kappa_ref,
    mix,
    wide,
    tri_x,
    sent_x,
    got_x,
    forcing,
    ports_t,
    ports_h,
    exp_high,
    exp_low,
    angle_cos,
    angle_sin,
    cos_high,
    cos_low,
    leg_high,
    leg_low,
    flip_high,
    flip_low,
    sent_n,
    got_n,
    spread_n,
    shell_q,
    partial,
    green,
    solved,
    port_y,
    const_z,
    const_y,
    relay_sem,
    load_sem,
    x_send,
    x_recv,
    n_send,
    n_recv,
    u_send,
    u_recv,
    py_send,
    py_recv,
    cz_send,
    cz_recv,
    cy_send,
    cy_recv,
):
    row, mode = lax.axis_index("row"), lax.axis_index("lm")
    y, z, core = row // 16, lax.rem(row // 2, 8), lax.rem(row, 2)
    other = row + 1 - 2 * core
    turn = [lax.rem(mode + d, 4) for d in range(4)]
    x_peers = [(row, turn[d]) for d in (2, 1, 3)]
    core_peers = [(other, turn[d]) for d in (2, 1, 3, 0)]

    loads = [
        pltpu.make_async_copy(state_hbm, state_raw, load_sem.at[0]),
        pltpu.make_async_copy(previous_hbm, previous_raw, load_sem.at[1]),
        pltpu.make_async_copy(below_hbm, sides_raw.at[0], load_sem.at[2]),
        pltpu.make_async_copy(above_hbm, sides_raw.at[1], load_sem.at[3]),
        pltpu.make_async_copy(kappa_hbm, kappa_ref, load_sem.at[4]),
    ]
    for load in loads:
        load.start()

    def along_z(d):
        return (y * 16 + lax.rem(z + d, 8) * 2 + core, mode)

    def along_y(d):
        return (lax.rem(y + d, 8) * 16 + z * 2 + core, mode)

    z_peers = [along_z(d) for d in (4, 3, 5, 2, 6, 1, 7)]
    y_peers = [along_y(d) for d in (4, 3, 5, 2, 6, 1, 7)]

    barrier = pltpu.get_barrier_semaphore()
    near = x_peers + core_peers + [line(d) for line in (along_z, along_y) for d in (1, 7)]
    for peer in near:
        pl.semaphore_signal(barrier, inc=1, device_id=peer, device_id_type=MESH)

    def relay(step):
        for k, line in enumerate((along_z, along_y)):
            for side, d in enumerate((step, 8 - step)):
                pl.semaphore_signal(
                    relay_sem.at[step - 1, k, side],
                    inc=1,
                    device_id=line(d),
                    device_id_type=MESH,
                )

    def relayed(step):
        for k in range(2):
            for side in range(2):
                pl.semaphore_wait(relay_sem.at[step - 1, k, side], 1)

    def send(source, target, send_sem, recv_sem, peer):
        copy = pltpu.make_async_remote_copy(
            src_ref=source,
            dst_ref=target,
            send_sem=send_sem,
            recv_sem=recv_sem,
            device_id=peer,
            device_id_type=MESH,
        )
        copy.start()
        return copy

    def receive(copies):
        for copy in copies:
            copy.wait_recv()

    source_id, target_id = iota((256, 256), 0), iota((256, 256), 1)
    part = (source_id == 2 * (target_id & 127) + (target_id >> 7)).astype(F32).astype(BF16)
    unite = (target_id == 2 * (source_id & 127) + (source_id >> 7)).astype(F32).astype(BF16)
    sub, lane = iota(TILE, 0), iota(TILE, 1)
    parity, field = sub >> 2, sub & 3
    degree = (mode * 256 + 2 * lane + parity).astype(F32)
    scale = jnp.sqrt(degree + 0.5)

    def to_tiles(values, target):
        for f in range(FIELDS):
            for p in range(2):
                target[pl.ds(p * 4 + f, SHELLS_DEV, stride=8), :] = values[
                    f * 16 : (f + 1) * 16, p * 128 : (p + 1) * 128
                ]

    def from_tiles(source):
        return jnp.concatenate(
            [
                jnp.concatenate(
                    [source[pl.ds(p * 4 + f, SHELLS_DEV, stride=8), :] for p in range(2)], axis=1
                )
                for f in range(FIELDS)
            ],
            axis=0,
        )

    def phase(order, shape):
        return order * (2 * iota(shape, 1) + 1)

    wide_shape = (8, HALF)
    for p, groups in ((0, 7), (1, 4)):
        for group in range(groups):
            turns = phase(32 * (group * 8 + iota(wide_shape, 0)) + p, wide_shape)
            angle_cos[p, group * 8 : group * 8 + 8, :] = 2.0 * cosine(turns)
            angle_sin[p, group * 8 : group * 8 + 8, :] = 2.0 * cosine(turns - NLAT)
    toeplitz = central_ratio(512 + iota((8, 640), 0) - iota((8, 640), 1))
    hankel = [central_ratio(iota((8, 1024), 0) + iota((8, 1024), 1) + p) for p in range(2)]
    for step in range(16):
        rows = slice(step * 8, step * 8 + 8)
        moved = toeplitz if step == 0 else pltpu.roll(toeplitz, step * 8, 1)
        for b in range(4):
            ports_t[b, rows, :] = moved[:, (4 - b) * 128 : (5 - b) * 128]
        for p in range(2):
            moved = hankel[p] if step == 0 else pltpu.roll(hankel[p], 1024 - step * 8, 1)
            for b in range(7):
                ports_h[p, b, rows, :] = moved[:, b * 128 : (b + 1) * 128]
    tri_x[...] = jnp.zeros_like(tri_x)
    spread_n[...] = jnp.zeros_like(spread_n)
    wide[...] = jnp.zeros_like(wide)
    loads[0].wait()
    to_tiles(permute_lanes(state_raw[...].reshape(48, 256), part), tri_x)
    wide[...] = (tri_x[...].reshape(SHELLS_DEV, 8, 128) * scale).reshape(128, 128)
    for k in range(4):
        for f in range(FIELDS):
            sent_x[k, f] = wide[pl.ds(k * 32 + f, 8, stride=4), :]
    pl.semaphore_wait(barrier, len(near))
    copies_x = [
        send(
            sent_x.at[peer[1]],
            got_x.at[mode],
            x_send.at[d],
            x_recv.at[d],
            peer,
        )
        for d, peer in enumerate(x_peers)
    ]
    relay(1)
    got_x[mode] = sent_x[mode]

    for p in range(2):
        for a in range(4):
            for b in range(4):
                here = (p, slice(a * 128, a * 128 + 128), slice(b * 128, b * 128 + 128))
                if b <= a:
                    high, low = split2(ports_t[a - b] * ports_h[p, a + b])
                else:
                    high = low = jnp.zeros((128, 128), BF16)
                exp_high[here] = high
                exp_low[here] = low

    base_shape = (16, HALF)
    turns = phase(2 * iota(base_shape, 0), base_shape)
    base_cos, base_sin = cosine(turns), cosine(turns - NLAT)
    def fill(q, unused):
        for p in range(2):
            row_cos, row_sin = angle_cos[p, pl.ds(q, 1), :], angle_sin[p, pl.ds(q, 1), :]
            values = row_cos * base_cos - row_sin * base_sin
            if p == 0:
                values = jnp.where((iota(base_shape, 0) + 16 * q) == 0, 1.0, values)
            high, low = split2(values)
            where = pl.ds(pl.multiple_of(q * 16, 16), 16)
            cos_high[p, where, :] = high
            cos_low[p, where, :] = low
        return unused

    lax.fori_loop(0, 32, fill, 0)
    order = (iota((16, 56), 0) + 16 * iota((16, 56), 1)).astype(F32)
    series = jnp.where(order > HALF, 0.0, -1.0 / (4.0 * order * order - 1.0))
    series = jnp.where(order == 0.0, 0.5, series)
    over_cos, over_sin = [
        jnp.dot(series, rows[0], precision=lax.Precision.HIGHEST, preferred_element_type=F32)
        for rows in (angle_cos, angle_sin)
    ]
    weight = jnp.sum(over_cos * base_cos - over_sin * base_sin, axis=0, keepdims=True)
    weight = weight * (2.0 / NLAT / 16.0)

    for p in range(2):
        for first in (0, 256):
            rows, depth = slice(first, first + 256), first + 256
            top, rest = exp_high[p, rows, :depth], exp_low[p, rows, :depth]
            both = dot(jnp.concatenate([top, rest], axis=0), cos_high[p, :depth, :])
            values = both[:256] + both[256:] + dot(top, cos_low[p, :depth, :])
            for part_of, table, flipped in zip(
                split2(values), (leg_high, leg_low), (flip_high, flip_low)
            ):
                table[p, rows, :] = part_of
                flipped[p, :, rows] = part_of.T

    receive(copies_x)
    even_rows = (iota((32, 1), 0) & 1) == 0
    sign = jnp.where(even_rows, 1.0, -1.0)

    def parities(left, right):
        return jnp.where(even_rows, left, right)

    def swap(values):
        rows = values.shape[0]
        return parities(pltpu.roll(values, rows - 1, 0), pltpu.roll(values, 1, 0))

    spectrum = jnp.concatenate([jnp.concatenate([got_x[k].reshape(24, 128), jnp.zeros(TILE, F32)], axis=0)
            for k in range(4)], axis=1)
    sides = parities(*[dot3(spectrum, leg_high[p], leg_low[p]) for p in range(2)])
    grid = swap(sides) + sign * sides
    velocity, magnetic, thermal = [grid[f * 8 : f * 8 + 8] * weight for f in range(FIELDS)]
    product = jnp.concatenate(
        [
            grid[8:16] * magnetic - grid[:8] * velocity,
            grid[:8] * magnetic,
            -(grid[:8] * thermal),
            jnp.zeros_like(thermal),
        ],
        axis=0,
    )
    folded = swap(product) + sign * product
    terms = parities(*[dot3(folded, flip_high[p], flip_low[p]) for p in range(2)])
    for k in range(4):
        sent_n[k] = terms[:24, k * 128 : (k + 1) * 128].reshape(FIELDS, 8, 128)
    mine = core * 4 + mode
    copies_n = [
        send(sent_n.at[peer[1]], got_n.at[mine], n_send.at[d], n_recv.at[d], peer)
        for d, peer in enumerate(x_peers[:1] + core_peers[:1] + x_peers[1:] + core_peers[1:])
    ]
    got_n[mine] = sent_n[mode]
    relayed(1)
    relay(2)

    loads[1].wait()
    to_tiles(permute_lanes(previous_raw[...].reshape(48, 256), part), wide)
    push = 4.0 * SHELLS_DEV * SHELLS_DEV
    forcing[pl.ds(core * SHELLS_DEV, SHELLS_DEV)] = (
        2.0 * tri_x[...] - (0.5 * push) * wide[...]
    ).reshape(SHELLS_DEV, 8, 128)
    copy_u = send(
        forcing.at[pl.ds(core * SHELLS_DEV, SHELLS_DEV)],
        forcing.at[pl.ds(core * SHELLS_DEV, SHELLS_DEV)],
        u_send.at[0],
        u_recv.at[0],
        core_peers[3],
    )

    loads[4].wait()
    kappa = jnp.full(TILE, 1.0, F32)
    for f in range(FIELDS):
        kappa = jnp.where(field == f, kappa_ref[f], kappa)
    alpha = 1.0 / (kappa * (16.0 * SHELLS_DEV * SHELLS_DEV))
    steep = 16.0 * (degree * (degree + 1.0))
    one = jnp.ones(TILE, F32)
    for block in range(SHELLS // 256):
        rho = (iota((256, 128), 0) + block * 256).astype(F32) + (SHELLS + 0.5)
        shell_q[block * 256 : (block + 1) * 256, :] = 1.0 / (rho * rho)

    def beta(shell):
        return alpha + steep * shell_q[pl.ds(shell, 1), :]

    first_shell = (row // 2) * CHIP
    grow, change = one, one
    back, back_change = one, one
    for s in range(CHIP):
        green[1, s] = grow
        change = beta(first_shell + s) * grow + change
        grow = grow + change
        t = CHIP - 1 - s
        green[0, t] = back
        back_change = beta(first_shell + t) * back + back_change
        back = back + back_change
    inverse = 1.0 / grow
    for s in range(CHIP):
        green[0, s] = green[0, s] * inverse
        green[1, s] = green[1, s] * inverse

    def line_ports(line):
        starts = [line * 256 + k * CHIP for k in range(8)]
        carry = []
        for start in starts:
            change = beta(start) + one
            carry += [one + change, change, one, one]

        def step(s, carry):
            after = []
            for k, start in enumerate(starts):
                grow, change, inner, inner_change = carry[4 * k : 4 * k + 4]
                here = beta(start + s)
                change = here * grow + change
                inner_change = here * inner + inner_change
                after += [grow + change, change, inner + inner_change, inner_change]
            return tuple(after)

        carry = lax.fori_loop(1, CHIP, step, tuple(carry))
        ports = []
        for k in range(8):
            grow, change, inner, _ = carry[4 * k : 4 * k + 4]
            tau = 1.0 / grow
            ports.append((inner * tau, tau, tau, (grow - change) * tau))
        return ports

    parts_z = level_parts(line_ports(y), z)
    port_y[y, 0], port_y[y, 1], port_y[y, 2] = parts_z[4][0], parts_z[4][1], parts_z[4][3]

    loads[2].wait()
    loads[3].wait()
    mix[...] = jnp.zeros_like(mix)
    for k in range(2):
        mix[k * 8 : k * 8 + FIELDS, :] = sides_raw[k, :, 0] + sides_raw[k, :, 1]
    parted = permute_lanes(mix[...], part)
    bottom, top = [
        jnp.concatenate([parted[k * 8 : k * 8 + 4, :128], parted[k * 8 : k * 8 + 4, 128:]], axis=0)
        for k in range(2)
    ]
    bottom, top = bottom * (SHELLS - 0.5), top * (2 * SHELLS + 0.5)

    relayed(2)
    copies_py = [
        send(port_y.at[y], port_y.at[y], py_send.at[d], py_recv.at[d], peer)
        for d, peer in enumerate(y_peers)
    ]

    receive([copy_u])
    receive(copies_n)
    for q in range(8):
        for f in range(FIELDS):
            spread_n[pl.ds(q * 32 + f, 8, stride=4), :] = got_n[q, f]
    factor = (1.5 * push) * scale
    sums = [[None] * 4, [None] * 4]
    for s in range(CHIP):
        rho = (first_shell + s).astype(F32) + (SHELLS + 0.5)
        value = (alpha * rho) * (forcing[s] + factor * spread_n[s * 8 : s * 8 + 8, :])
        solved[s] = value
        for k in range(2):
            term = green[k, s] * value
            old = sums[k][s % 4]
            sums[k][s % 4] = term if old is None else old + term
    for k in range(2):
        const_z[z, k] = (sums[k][0] + sums[k][1]) + (sums[k][2] + sums[k][3])
    copies_cz = [
        send(const_z.at[z], const_z.at[z], cz_send.at[d], cz_recv.at[d], peer)
        for d, peer in enumerate(z_peers)
    ]

    run = jnp.zeros(TILE, F32)
    for s in range(CHIP):
        run = run + (green[1, s] * grow) * solved[s]
        partial[s] = green[0, s] * run
    run = jnp.zeros(TILE, F32)
    for s in reversed(range(CHIP)):
        solved_here = solved[s]
        solved[s] = partial[s] + green[1, s] * run
        run = run + (green[0, s] * grow) * solved_here

    wide[...] = (
        spread_n[pl.ds(core * 128, 128), :].reshape(SHELLS_DEV, 8, 128) * scale
    ).reshape(128, 128)
    nonlinear_ref[...] = permute_lanes(from_tiles(wide), unite).reshape(FIELDS, SHELLS_DEV, 256)

    receive(copies_cz)
    total0, total1, lower_z, upper_z = level_constants(
        parts_z, [(const_z[k, 0], const_z[k, 1]) for k in range(8)], z
    )
    const_y[y, 0], const_y[y, 1] = total0, total1
    copies_cy = [
        send(const_y.at[y], const_y.at[y], cy_send.at[d], cy_recv.at[d], peer)
        for d, peer in enumerate(y_peers)
    ]

    own_shells = pl.ds(core * SHELLS_DEV, SHELLS_DEV)
    number = (row * SHELLS_DEV + iota((SHELLS_DEV, 8, 128), 0)).astype(F32) + (SHELLS + 0.5)
    over = 1.0 / number
    ordered = []
    for values in (
        solved[own_shells] * over - tri_x[...].reshape(SHELLS_DEV, 8, 128),
        green[0, own_shells] * over,
        green[1, own_shells] * over,
    ):
        wide[...] = values.reshape(128, 128)
        ordered.append(permute_lanes(from_tiles(wide), unite))

    receive(copies_py)
    parts_y = level_parts(
        [(port_y[k, 0], port_y[k, 1], port_y[k, 1], port_y[k, 2]) for k in range(8)], y
    )
    receive(copies_cy)
    _, _, lower_y, upper_y = level_constants(
        parts_y, [(const_y[k, 0], const_y[k, 1]) for k in range(8)], y
    )
    line_low = parts_y[2][0] * bottom + parts_y[2][1] * top + lower_y
    line_up = parts_y[3][0] * bottom + parts_y[3][1] * top + upper_y
    chip_low = parts_z[2][0] * line_low + parts_z[2][1] * line_up + lower_z
    chip_up = parts_z[3][0] * line_low + parts_z[3][1] * line_up + upper_z
    edges = [
        jnp.concatenate([tile[:4], tile[4:]], axis=1)
        for tile in (chip_low, chip_up, jnp.zeros(TILE, F32), jnp.zeros(TILE, F32))
    ]
    edges = permute_lanes(jnp.concatenate(edges, axis=0), unite)
    for f in range(FIELDS):
        rows = slice(f * SHELLS_DEV, (f + 1) * SHELLS_DEV)
        new_ref[f] = (
            ordered[0][rows]
            + ordered[1][rows] * edges[f : f + 1]
            + ordered[2][rows] * edges[4 + f : 5 + f]
        )

    for copy in copies_x + copies_n + [copy_u] + copies_py + copies_cz + copies_cy:
        copy.wait_send()


def write_out(new_ref, nonlinear_ref, new_hbm, nonlinear_hbm, sem):
    copies = [
        pltpu.make_async_copy(new_ref, new_hbm, sem.at[0]),
        pltpu.make_async_copy(nonlinear_ref, nonlinear_hbm, sem.at[1]),
    ]
    for copy in copies:
        copy.start()
    for copy in copies:
        copy.wait()


def local(state, previous_terms, below, above, kappa):
    block = jax.ShapeDtypeStruct(state.shape, F32)
    vmem, dma = pltpu.VMEM, pltpu.SemaphoreType.DMA
    anywhere = pl.BlockSpec(memory_space=pl.ANY)
    inside = pl.BlockSpec(memory_space=pltpu.VMEM)
    scratch = [
        vmem((FIELDS, SHELLS_DEV, 256), F32),
        vmem((FIELDS, SHELLS_DEV, 256), F32),
        vmem((2, FIELDS, 2, 256), F32),
        pltpu.SMEM((FIELDS,), F32),
        vmem((16, 256), F32),
        vmem((128, 128), F32),
        vmem((128, 128), F32),
        vmem((4, FIELDS, 8, 128), F32),
        vmem((4, FIELDS, 8, 128), F32),
        vmem((CHIP, 8, 128), F32),
        vmem((4, 128, 128), F32),
        vmem((2, 7, 128, 128), F32),
        vmem((2, PAIRS, PAIRS), BF16),
        vmem((2, PAIRS, PAIRS), BF16),
        vmem((2, 56, HALF), F32),
        vmem((2, 56, HALF), F32),
        vmem((2, PAIRS, HALF), BF16),
        vmem((2, PAIRS, HALF), BF16),
        vmem((2, PAIRS, HALF), BF16),
        vmem((2, PAIRS, HALF), BF16),
        vmem((2, HALF, PAIRS), BF16),
        vmem((2, HALF, PAIRS), BF16),
        vmem((4, FIELDS, 8, 128), F32),
        vmem((8, FIELDS, 8, 128), F32),
        vmem((CHIP * 8, 128), F32),
        vmem((SHELLS, 128), F32),
        vmem((CHIP, 8, 128), F32),
        vmem((2, CHIP, 8, 128), F32),
        vmem((CHIP, 8, 128), F32),
        vmem((8, 3, 8, 128), F32),
        vmem((8, 2, 8, 128), F32),
        vmem((8, 2, 8, 128), F32),
        pltpu.SemaphoreType.REGULAR((2, 2, 2)),
        dma((5,)),
        dma((3,)),
        dma((3,)),
        dma((7,)),
        dma((7,)),
        dma((1,)),
        dma((1,)),
    ] + [dma((7,))] * 6
    held = pltpu.VMEM(state.shape, F32)
    operands = [
        pltpu.with_memory_space_constraint(operand, pltpu.HBM)
        for operand in (
            state,
            previous_terms,
            jnp.transpose(below, (1, 0, 2)),
            jnp.transpose(above, (1, 0, 2)),
            kappa,
        )
    ]
    results = pl.pallas_call(
        kernel,
        out_shape=(held, held),
        in_specs=[anywhere] * 5,
        out_specs=(inside, inside),
        scratch_shapes=scratch,
        compiler_params=pltpu.CompilerParams(
            collective_id=0, has_side_effects=True, vmem_limit_bytes=32 * 1024 * 1024
        ),
    )(*operands)
    return pl.pallas_call(
        write_out,
        out_shape=(block, block),
        in_specs=[inside] * 2,
        out_specs=(anywhere, anywhere),
        scratch_shapes=[dma((2,))],
    )(*[pltpu.with_memory_space_constraint(result, pltpu.VMEM) for result in results])


def solution(mesh):
    in_specs = (
        P(None, "row", "lm"),
        P(None, "row", "lm"),
        P(None, None, "lm"),
        P(None, None, "lm"),
        P(),
    )
    out_specs = (P(None, "row", "lm"), P(None, "row", "lm"))
    return jax.shard_map(local, mesh=mesh, in_specs=in_specs, out_specs=out_specs, check_vma=False)
```
